128 devices in a mesh: grp: 16 (over x_hi, y, core), head: 8 (over x_lo, z).
Axes of the slice: x: 4 (x_hi: 2, x_lo: 2; x = x_hi * 2 + x_lo), y: 4, z: 4, core: 2. Of those that a mesh axis runs over, the one named last changes fastest.
Arguments:
- query: bfloat16 [512, 8192], P('grp', 'head'), may hold values from -160 to 160
- new_key: bfloat16 [512, 1024], P('grp', 'head'), may hold values from -6 to 6
- new_value: bfloat16 [512, 1024], P('grp', 'head'), may hold values from -6 to 6
- key_cache: bfloat16 [512, 8, 1024, 128], P('grp', 'head'), may hold values from -6 to 6
- value_cache: bfloat16 [512, 8, 1024, 128], P('grp', 'head'), may hold values from -6 to 6
- lengths: int32 [512], P('grp'), may hold values from 1 to 1024, 262144 in all
- slot_row: int32 [512], replicated, may hold values from 0 to 511, each once
- resid: bfloat16 [512, 8192], P(None, 'grp'), may hold values from -10 to 10
- out_weight: bfloat16 [8192, 8192], P('head', 'grp'), may hold values from -0.5 to 0.5
- norm_gain: bfloat16 [8192], P('grp'), may hold values from 0.5 to 1.5
- gate_weight: bfloat16 [8192, 28672], P(None, ('grp', 'head')), may hold values from -0.0625 to 0.0625
- up_weight: bfloat16 [8192, 28672], P(None, ('grp', 'head')), may hold values from -0.0625 to 0.0625
- down_weight: bfloat16 [28672, 8192], P(('grp', 'head')), may hold values from -0.125 to 0.125
Outputs:
- residual_out: bfloat16 [512, 8192], P(None, ('grp', 'head'))
- layer_out: bfloat16 [512, 8192], P(None, ('grp', 'head'))
The draws below stay inside these ranges and needn't reach their ends.
Inputs may be any that keep to these rules, and one draw needn't show every extreme that they name: `lengths`: each row attends to its cache slots below its length and to its own new key. `slot_row`: A permutation of the rows.
All inputs are finite; a program needn't handle non-finite values. No bound on the sum of `lengths` on one device may be relied on, other than what follows from the above.
Results may differ from the reference program's by a relative error of at most 0.015.
Values may be sent and summed in bfloat16 or wider, within the bound.
A program may use at most 128 MiB of HBM per device.

```python
import math
import jax
import jax.numpy as jnp
import numpy as np
from jax import lax

D = 8192
FF = 28672
HQ = 64
KVH = 8
HD = 128
CTX = 1024
ROWS = 512


def anchor_keys(key):
    return jnp.clip(jax.random.normal(key, (ROWS, KVH, HD), jnp.float32), -4.0, 4.0)


def draw_key_cache(key, part):
    anchors = anchor_keys(key)
    key = jax.random.fold_in(key, 11)
    base_draw = jnp.clip(jax.random.normal(key, (ROWS, KVH, CTX, HD), jnp.float32), -6.0, 6.0)
    joined = jnp.concatenate([anchors[:, :, None, :], base_draw[:, :, 1:, :]], axis=2)
    return joined.astype(jnp.bfloat16)


def draw_new_key(key, part):
    key = jax.random.fold_in(key, 12)
    base_draw = jnp.clip(jax.random.normal(key, (ROWS, KVH * HD), jnp.float32), -6.0, 6.0)
    return base_draw.astype(jnp.bfloat16)


def draw_query(key, part):
    key = jax.random.fold_in(key, 13)
    base_draw = jnp.clip(jax.random.normal(key, (ROWS, HQ * HD), jnp.float32), -6.0, 6.0)
    return base_draw.astype(jnp.bfloat16)


def draw_resid(key, part):
    key = jax.random.fold_in(key, 14)
    row_key, col_key, base_key = jax.random.split(key, 3)
    row_scale = jnp.exp(jax.random.uniform(row_key, (ROWS, 1), jnp.float32, jnp.log(0.05), jnp.log(0.5)))
    col_rough = jnp.exp(jax.random.uniform(col_key, (1, D), jnp.float32, jnp.log(0.7), jnp.log(1.4)))
    position = jnp.arange(D, dtype=jnp.float32)[None, :] / D
    base_draw = jnp.clip(jax.random.normal(base_key, (ROWS, D), jnp.float32), -6.0, 6.0)
    col_scale = col_rough * jnp.exp(jnp.log(3.0) * position)
    return jnp.clip(base_draw * row_scale * col_scale, -10.0, 10.0).astype(jnp.bfloat16)


def spiked(drawn, stream_key, source, target, parts, factor):
    owner, partner = [(jnp.arange(drawn.shape[dim]) // (drawn.shape[dim] // parts)).reshape([-1 if axis == dim else 1 for axis in range(drawn.ndim)]) for dim in (source, target)]
    chosen = jax.random.permutation(stream_key, parts)[partner]
    strong = (owner == chosen) | (owner == (partner + parts // 2) % parts)
    return jnp.where(strong, factor * drawn, drawn)


def steps_of(own_key, dims, cuts, low, largest):
    loudness, own = 1.0, jax.random.fold_in(own_key, 6)
    for axis_at, blocks in cuts:
        draws = jnp.exp(jax.random.uniform(jax.random.fold_in(own, axis_at), (blocks,), jnp.float32, low / len(cuts), largest / len(cuts)))
        loudness = loudness * jnp.repeat(draws, dims[axis_at] // blocks).reshape([-1 if axis == axis_at else 1 for axis in range(len(dims))])
    return loudness


def profile(number_of, total, most, lean):
    loads = [(1 << 20) // math.isqrt(standing ** lean) + 1 for standing in range(2, number_of + 1)]
    rest, holding = total - most - (number_of - 1), [1] * (number_of - 1)
    while rest > 0:
        candidates = [i for i in range(number_of - 1) if holding[i] < most]
        whole, left = sum([loads[i] for i in candidates]), rest
        for i in candidates:
            extra = min(most - holding[i], max(1, left * loads[i] // whole), rest)
            holding[i] = holding[i] + extra
            rest = rest - extra
    return np.array([most] + holding)


def uneven(stream_key, number_of, total, most, lean):
    if number_of == 2:
        one = jax.random.randint(stream_key, (), max(1, total - most), min(most, total - 1) + 1)
        return jnp.stack([one, total - one])
    sizes = jnp.asarray(profile(number_of, total, most, lean), jnp.int32)
    twos = (number_of - 1) // 2
    donor, sink = sizes[1:1 + 2 * twos:2], sizes[2:2 + 2 * twos:2]
    slack = jnp.minimum(donor - 1, most - sink)
    moved = jax.random.randint(jax.random.fold_in(stream_key, 1), (twos,), 0, 1 << 20) % (slack + 1)
    sizes = sizes.at[1:1 + 2 * twos:2].set(donor - moved).at[2:2 + 2 * twos:2].set(sink + moved)
    return sizes[jax.random.permutation(jax.random.fold_in(stream_key, 2), number_of)]


def scatter_about(own_key, extent, spread, most, cuts=(), held_as=jnp.bfloat16):
    values = jax.random.normal(own_key, extent, jnp.float32) * spread
    if len(cuts) > 0:
        values = steps_of(own_key, extent, cuts, -0.22, 0.18) * values
    return jnp.clip(values, min=-most, max=most).astype(held_as)


def heavy_noise(key, shape, scale, limit, cuts, heavy, held_as=jnp.bfloat16):
    drawn = scale * jax.random.normal(key, shape, jnp.float32)
    if cuts:
        drawn = drawn * steps_of(key, shape, cuts, -0.22, 0.18)
    return jnp.clip(spiked(drawn, jax.random.fold_in(key, 3), *heavy), -limit, limit).astype(held_as)


def setup_inputs(seed: int = 0) -> dict:
    splits = jax.random.split(jax.random.key(seed), 14)
    query = draw_query(jax.random.fold_in(splits[13], 71), 0)
    new_key = draw_new_key(jax.random.fold_in(splits[13], 71), 0)
    new_value = scatter_about(splits[2], (ROWS, KVH * HD), 1.0, 6.0, ((0, 16), (1, 8)))
    key_cache = draw_key_cache(jax.random.fold_in(splits[13], 71), 0)
    value_cache = scatter_about(splits[4], (ROWS, KVH, CTX, HD), 1.0, 6.0, ((0, 16), (1, 8)))
    lengths = uneven(splits[5], ROWS, ROWS * CTX // 2, CTX, 2).astype(jnp.int32)
    slot_row = jax.random.permutation(splits[6], ROWS).astype(jnp.int32)
    resid = draw_resid(jax.random.fold_in(splits[13], 71), 0)
    out_weight = scatter_about(splits[8], (HQ * HD, D), HD ** -0.5, 0.5, ((0, 8), (1, 16)))
    norm_gain = jnp.clip(1.0 + 0.1 * jax.random.normal(splits[9], (D,), jnp.float32), 0.5, 1.5).astype(jnp.bfloat16)
    gate_weight = scatter_about(splits[10], (D, FF), D ** -0.5, 0.0625, ((1, 128),))
    up_weight = scatter_about(splits[11], (D, FF), D ** -0.5, 0.0625, ((1, 128),))
    down_weight = heavy_noise(splits[12], (FF, D), FF ** -0.5, 0.125, ((0, 128),), (0, 1, 128, 5.5))
    return {"query": query, "new_key": new_key, "new_value": new_value, "key_cache": key_cache, "value_cache": value_cache, "lengths": lengths, "slot_row": slot_row, "resid": resid, "out_weight": out_weight, "norm_gain": norm_gain, "gate_weight": gate_weight, "up_weight": up_weight, "down_weight": down_weight}


def attend_row(inputs):
    row_query, row_key, row_value, cache_keys, cache_values, row_length = inputs
    per_kv = HQ // KVH
    query_heads = row_query.astype(jnp.float32).reshape(KVH, per_kv, HD)
    score_scale = HD ** (-0.5)
    scores = jnp.einsum('jqd,jpd->jqp', query_heads, cache_keys.astype(jnp.float32)) * score_scale
    own_score = jnp.einsum('jqd,jd->jq', query_heads, row_key.astype(jnp.float32).reshape(KVH, HD)) * score_scale
    live_mask = jnp.arange(CTX, dtype=jnp.int32) < row_length
    scores = jnp.where(live_mask[None, None, :], scores, -1e+30)
    row_top = jnp.maximum(lax.optimization_barrier(jnp.max(scores, axis=2)), own_score)
    exp_scores = jnp.where(live_mask[None, None, :], jnp.exp(scores - row_top[:, :, None]), 0.0)
    exp_own = jnp.exp(own_score - row_top)
    weight_sum = lax.optimization_barrier(jnp.sum(exp_scores, axis=2)) + exp_own
    weights = (exp_scores / weight_sum[:, :, None]).astype(jnp.bfloat16)
    own_weight = (exp_own / weight_sum).astype(jnp.bfloat16)
    mixed_values = jnp.einsum('jqp,jpd->jqd', weights.astype(jnp.float32), cache_values.astype(jnp.float32))
    mixed_values = mixed_values + own_weight.astype(jnp.float32)[:, :, None] * row_value.astype(jnp.float32).reshape(KVH, 1, HD)
    return mixed_values.reshape(HQ * HD).astype(jnp.bfloat16)

def reference(query, new_key, new_value, key_cache, value_cache, lengths, slot_row, resid, out_weight, norm_gain, gate_weight, up_weight, down_weight):
    attended = lax.map(attend_row, (query, new_key, new_value, key_cache, value_cache, lengths))
    inverse = jnp.zeros((ROWS,), jnp.int32).at[slot_row].set(jnp.arange(ROWS, dtype=jnp.int32))
    ordered = attended[inverse]
    stream = resid.astype(jnp.float32) + jnp.dot(ordered, out_weight, preferred_element_type=jnp.float32)
    residual_out = stream.astype(jnp.bfloat16)
    mean_square = lax.optimization_barrier(jnp.mean(stream * stream, axis=1))
    normed = (stream * lax.rsqrt(mean_square + 1e-05)[:, None] * norm_gain.astype(jnp.float32)).astype(jnp.bfloat16)
    gate_acc = jnp.dot(normed, gate_weight, preferred_element_type=jnp.float32)
    up_acc = jnp.dot(normed, up_weight, preferred_element_type=jnp.float32)
    hidden = (jax.nn.silu(gate_acc) * up_acc).astype(jnp.bfloat16)
    layer_out = jnp.dot(hidden, down_weight, preferred_element_type=jnp.float32).astype(jnp.bfloat16)
    return (residual_out, layer_out)
```

```python
import jax
import jax.numpy as jnp
from jax import lax
from jax.experimental import pallas as pl
from jax.experimental.pallas import tpu as pltpu
from jax.sharding import PartitionSpec as P

D = 8192
HQ = 64
KVH = 8
HID = 224
MESH = pl.DeviceIdType.MESH
BF16 = jnp.bfloat16
F32 = jnp.float32

GATHER_LANES = ((0, 384), (384, 384), (768, 256))
GATHER_ORDER = ("xzy", "yxz", "zyx")
SCATTER_ROWS = ((0, 96), (96, 96), (192, 64))
SCATTER_ORDER = ("yzx", "zxy", "xyz")


def attend_local(query, new_key, new_value, key_cache, value_cache, lengths):
    rows_here, kv_here, cache_len, head_size = key_cache.shape
    per_kv = HQ // KVH
    query_heads = query.reshape(rows_here, kv_here, per_kv, head_size)
    score_scale = head_size ** (-0.5)
    scores = (
        jnp.einsum("rjqd,rjpd->rjqp", query_heads, key_cache, preferred_element_type=jnp.float32)
        * score_scale
    )
    own_score = (
        jnp.einsum(
            "rjqd,rjd->rjq",
            query_heads,
            new_key.reshape(rows_here, kv_here, head_size),
            preferred_element_type=jnp.float32,
        )
        * score_scale
    )
    live_mask = (jnp.arange(cache_len, dtype=jnp.int32)[None, :] < lengths[:, None])[
        :, None, None, :
    ]
    scores = jnp.where(live_mask, scores, -1e30)
    row_top = jnp.maximum(jnp.max(scores, axis=3), own_score)
    exp_scores = jnp.where(live_mask, jnp.exp(scores - row_top[..., None]), 0.0)
    exp_own = jnp.exp(own_score - row_top)
    weight_sum = jnp.sum(exp_scores, axis=3) + exp_own
    weights = (exp_scores / weight_sum[..., None]).astype(jnp.bfloat16)
    own_weight = (exp_own / weight_sum).astype(jnp.bfloat16)
    mixed_values = jnp.einsum(
        "rjqp,rjpd->rjqd", weights, value_cache, preferred_element_type=jnp.float32
    )
    own_values = new_value.reshape(rows_here, kv_here, 1, head_size).astype(jnp.float32)
    mixed_values = mixed_values + own_weight.astype(jnp.float32)[..., None] * own_values
    return mixed_values.reshape(rows_here, kv_here * per_kv * head_size).astype(jnp.bfloat16)


def device_at(x, y, z, c):
    return ((x // 2) * 8 + y * 2 + c, (x % 2) * 4 + z)


def block_index(where):
    x, y, z = where["x"], where["y"], where["z"]
    if x is None:
        xl, xh = slice(None), slice(None)
    else:
        xl, xh = x % 2, x // 2
    return (xl, slice(None) if z is None else z, xh, slice(None) if y is None else y)


def kept_index(where, kept):
    index = ()
    if "x" in kept:
        index += (where["x"] % 2,)
    if "z" in kept:
        index += (where["z"],)
    if "x" in kept:
        index += (where["x"] // 2,)
    if "y" in kept:
        index += (where["y"],)
    return index


def kept_shape(kept):
    shape = ()
    if "x" in kept:
        shape += (2,)
    if "z" in kept:
        shape += (4,)
    if "x" in kept:
        shape += (2,)
    if "y" in kept:
        shape += (4,)
    return shape


def layer_kernel(
    att, gain, slots, resid, out_w, gate_w, up_w, down_w,
    res_out, lay_out,
    gains, got_att, resid_own, resid_sib, ow_own, ow_sib,
    gate_own, gate_sib, up_own, up_sib, down_own, down_sib,
    proj, proj_got, xs, ys, acc_go, acc_gs, acc_uo, acc_us, square,
    perm, slot_col, hid_own, hid_sib, res_z, lay_z, res_rows,
    *rest,
):
    landing = [[rest[k * 3 + s] for s in range(3)] for k in range(3)]
    (load_sem, swap_s, swap_r, att_s, att_r, gain_s, gain_r, proj_s, proj_r,
     ga_s, ga_r, sc_s, sc_r, fin_s, fin_r) = rest[9:]

    g = lax.axis_index("grp")
    h = lax.axis_index("head")
    xh, y, c = g // 8, (g // 2) % 4, g % 2
    xl, z = h // 4, h % 4
    me = {"x": xh * 2 + xl, "y": y, "z": z}

    def on_axis(axis, step):
        place = dict(me)
        place[axis] = (me[axis] + step) % 4
        return place

    def at(place, core):
        return device_at(place["x"], place["y"], place["z"], core)

    sibling = at(me, 1 - c)
    loads = []
    for i, (src, dst) in enumerate(
        ((out_w, ow_own), (resid, resid_own), (gate_w, gate_own), (up_w, up_own), (down_w, down_own))
    ):
        copy = pltpu.make_async_copy(src, dst, load_sem.at[i])
        copy.start()
        loads.append(copy)

    barrier = pltpu.get_barrier_semaphore()
    partners = []
    for i in range(1, 16):
        partners.append(((g + i) % 16, h))
    for i in range(1, 8):
        partners.append((g, (h + i) % 8))
    partners.append(((g + 8) % 16, (h + 4) % 8))
    for partner in partners:
        pl.semaphore_signal(barrier, inc=1, device_id=partner, device_id_type=MESH)
    pl.semaphore_wait(barrier, len(partners))

    att_copies = []
    for i in range(1, 8):
        xy = (xh * 4 + y + i) % 8
        copy = pltpu.make_async_remote_copy(
            src_ref=att,
            dst_ref=got_att.at[xh * 4 + y],
            send_sem=att_s.at[i - 1],
            recv_sem=att_r.at[i - 1],
            device_id=((xy // 4) * 8 + (xy % 4) * 2 + c, h),
            device_id_type=MESH,
        )
        copy.start()
        att_copies.append(copy)
    got_att[xh * 4 + y] = att[...]
    swaps = []
    for i, (src, dst) in enumerate(
        ((out_w, ow_sib), (resid, resid_sib), (gate_w, gate_sib), (up_w, up_sib), (down_w, down_sib))
    ):
        copy = pltpu.make_async_remote_copy(
            src_ref=src, dst_ref=dst, send_sem=swap_s.at[i], recv_sem=swap_r.at[i],
            device_id=sibling, device_id_type=MESH,
        )
        copy.start()
        swaps.append(copy)
    gain_copies = []
    for i in range(1, 16):
        copy = pltpu.make_async_remote_copy(
            src_ref=gain,
            dst_ref=gains.at[g],
            send_sem=gain_s.at[i - 1],
            recv_sem=gain_r.at[i - 1],
            device_id=((g + i) % 16, h),
            device_id_type=MESH,
        )
        copy.start()
        gain_copies.append(copy)
    gains[g] = gain[...]

    slot_line = slots[0:1, :]
    for t in range(4):
        tile = jnp.broadcast_to(slot_line[:, t * 128:(t + 1) * 128].astype(F32), (128, 128))
        slot_col[t * 128:(t + 1) * 128, :] = tile.T
        batch = lax.broadcasted_iota(jnp.int32, (128, 512), 0) + t * 128
        perm[t * 128:(t + 1) * 128, :] = jnp.where(batch == slot_line, 1.0, 0.0).astype(BF16)
    square[...] = jnp.zeros_like(square)
    acc_go[...] = jnp.zeros_like(acc_go)
    acc_gs[...] = jnp.zeros_like(acc_gs)
    acc_uo[...] = jnp.zeros_like(acc_uo)
    acc_us[...] = jnp.zeros_like(acc_us)

    loads[1].wait()
    swaps[1].wait()
    my_slots = slot_col[pl.ds(pl.multiple_of((2 * h + c) * 32, 32), 32), :]
    lane = lax.broadcasted_iota(jnp.int32, (32, 128), 1).astype(F32)
    pick = jnp.concatenate(
        [jnp.where(my_slots == lane + 128.0 * t, 1.0, 0.0).astype(BF16) for t in range(4)], axis=1
    )

    @pl.when(c == 0)
    def _():
        res_rows[:, 0:512] = jnp.dot(pick, resid_own[...], preferred_element_type=F32)
        res_rows[:, 512:1024] = jnp.dot(pick, resid_sib[...], preferred_element_type=F32)

    @pl.when(c == 1)
    def _():
        res_rows[:, 0:512] = jnp.dot(pick, resid_sib[...], preferred_element_type=F32)
        res_rows[:, 512:1024] = jnp.dot(pick, resid_own[...], preferred_element_type=F32)

    loads[0].wait()
    swaps[0].wait()
    for copy in att_copies:
        copy.wait()
    rows = got_att[...].reshape(256, 1024)
    own_part = jnp.dot(rows, ow_own[...], preferred_element_type=F32).astype(BF16)
    sib_part = jnp.dot(rows, ow_sib[...], preferred_element_type=F32).astype(BF16)
    proj[:, :, pl.ds(pl.multiple_of(c * 512, 512), 512)] = own_part.reshape(8, 32, 512)
    proj[:, :, pl.ds(pl.multiple_of((1 - c) * 512, 512), 512)] = sib_part.reshape(8, 32, 512)
    proj_copies = []
    for i in range(1, 8):
        head = (h + i) % 8
        copy = pltpu.make_async_remote_copy(
            src_ref=proj.at[head],
            dst_ref=proj_got.at[i - 1],
            send_sem=proj_s.at[i - 1],
            recv_sem=proj_r.at[i - 1],
            device_id=(g, head),
            device_id_type=MESH,
        )
        copy.start()
        proj_copies.append(copy)
    total = res_rows[...] + proj[h].astype(F32)
    for i in range(7):
        proj_copies[i].wait()
        total = total + proj_got[i].astype(F32)
    mine = block_index(me)
    xs[mine] = total.astype(BF16)

    def gather_stage(k, s):
        order = GATHER_ORDER[k]
        start, width = GATHER_LANES[k]
        lanes = pl.ds(start, width)
        done = order[:s]
        src_place = {a: (None if a in done else me[a]) for a in "xyz"}
        src = xs.at[(*block_index(src_place), slice(None), lanes)]
        copies = []
        for d in range(1, 4):
            copy = pltpu.make_async_remote_copy(
                src_ref=src, dst_ref=src,
                send_sem=ga_s.at[k, s, d - 1], recv_sem=ga_r.at[k, s, d - 1],
                device_id=at(on_axis(order[s], d), c), device_id_type=MESH,
            )
            copy.start()
            copies.append(copy)
        return copies

    def gather_wait(k, s, copies):
        order = GATHER_ORDER[k]
        start, width = GATHER_LANES[k]
        lanes = pl.ds(start, width)
        done = order[:s]
        for d in range(1, 4):
            place = on_axis(order[s], 4 - d)
            place = {a: (None if a in done else place[a]) for a in "xyz"}
            dst = xs.at[(*block_index(place), slice(None), lanes)]
            pltpu.make_async_remote_copy(
                src_ref=dst, dst_ref=dst,
                send_sem=ga_s.at[k, s, d - 1], recv_sem=ga_r.at[k, s, d - 1],
                device_id=at(on_axis(order[s], d), c), device_id_type=MESH,
            ).wait_recv()

    stages = [[None] * 3 for _ in range(3)]
    for k in range(3):
        stages[k][0] = gather_stage(k, 0)
    for s in range(2):
        for k in range(3):
            gather_wait(k, s, stages[k][s])
            stages[k][s + 1] = gather_stage(k, s + 1)

    for i in (2, 3):
        loads[i].wait()
        swaps[i].wait()
    for copy in gain_copies:
        copy.wait()
    for k in range(3):
        gather_wait(k, 2, stages[k][2])
        start, width = GATHER_LANES[k]

        def feed(block, _, start=start, width=width):
            bxh, by = block // 4, block % 4
            pieces = []
            sums = square[...]
            for t in range(start // 128, (start + width) // 128):
                part = xs[:, :, bxh, by, :, t * 128:(t + 1) * 128].reshape(256, 128).astype(F32)
                sums = sums + part * part
                scale = gains[2 * block + t // 4, t % 4:t % 4 + 1, :]
                pieces.append((part * scale).astype(BF16))
            square[...] = sums
            scaled = jnp.concatenate(pieces, axis=1)
            depth = pl.ds(pl.multiple_of(block * 1024 + start, 128), width)
            for acc, weight in (
                (acc_go, gate_own), (acc_gs, gate_sib), (acc_uo, up_own), (acc_us, up_sib)
            ):
                acc[...] += jnp.dot(scaled, weight[depth, :], preferred_element_type=F32)
            return 0

        lax.fori_loop(0, 8, feed, 0)

    norm = lax.rsqrt(jnp.sum(square[...], axis=1, keepdims=True) / D + 1e-05)
    for acc_g, acc_u, hid in ((acc_go, acc_uo, hid_own), (acc_gs, acc_us, hid_sib)):
        gate = acc_g[...] * norm
        hid[...] = (gate * jax.nn.sigmoid(gate) * (acc_u[...] * norm)).astype(BF16)

    lane_low = lax.broadcasted_iota(jnp.int32, (256, 128), 1) < 64
    odd = h % 2
    tiles = []
    for core in range(2):
        window = pl.ds(pl.multiple_of(core * 512 + (h // 2) * 128, 128), 128)
        tiles.append(xs[:, :, xh, y, :, window].reshape(256, 128).astype(F32))
    even_pack = jnp.where(lane_low, tiles[0], pltpu.roll(tiles[1], 64, 1))
    odd_pack = jnp.where(lane_low, pltpu.roll(tiles[0], 64, 1), tiles[1])
    packed = jnp.where(odd == 0, even_pack, odd_pack)
    res_z[:, c] = packed.astype(BF16).reshape(8, 32, 128)
    res_copy = pltpu.make_async_remote_copy(
        src_ref=res_z.at[:, c], dst_ref=res_z.at[:, c], send_sem=fin_s.at[0], recv_sem=fin_r.at[0],
        device_id=sibling, device_id_type=MESH,
    )
    res_copy.start()

    loads[4].wait()
    swaps[4].wait()

    def project(block, _):
        bxh, by = block // 4, block % 4
        col = pl.ds(pl.multiple_of(block * 1024, 1024), 1024)
        wide = jnp.dot(hid_own[...], down_own[:, col], preferred_element_type=F32)
        wide = wide + jnp.dot(hid_sib[...], down_sib[:, col], preferred_element_type=F32)
        for pair in range(4):
            low = wide[:, pair * 128:(pair + 1) * 128]
            high = wide[:, 512 + pair * 128:512 + (pair + 1) * 128]
            first = jnp.where(lane_low, low, pltpu.roll(high, 64, 1)).astype(BF16)
            second = jnp.where(lane_low, pltpu.roll(low, 64, 1), high).astype(BF16)
            ys[pair // 2, (pair % 2) * 2, bxh, by] = first
            ys[pair // 2, (pair % 2) * 2 + 1, bxh, by] = second
        return 0

    lax.fori_loop(0, 8, project, 0)

    def scatter_stage(k, s):
        order = SCATTER_ORDER[k]
        start, count = SCATTER_ROWS[k]
        axis = order[s]
        copies = []
        for d in range(1, 4):
            target = on_axis(axis, d)
            place = {a: (None if a in order[s + 1:] else target[a]) for a in "xyz"}
            copy = pltpu.make_async_remote_copy(
                src_ref=ys.at[(*block_index(place), pl.ds(start, count))],
                dst_ref=landing[k][s].at[d - 1],
                send_sem=sc_s.at[k, s, d - 1], recv_sem=sc_r.at[k, s, d - 1],
                device_id=at(target, c), device_id_type=MESH,
            )
            copy.start()
            copies.append(copy)
        return copies

    def scatter_sum(k, s, copies):
        order = SCATTER_ORDER[k]
        start, count = SCATTER_ROWS[k]
        for copy in copies:
            copy.wait_recv()
        kept = order[s + 1:]

        def add(block, _):
            place = dict(me)
            for i, a in enumerate(kept):
                place[a] = (block // 4**i) % 4
            spot = (*block_index(place), pl.ds(start, count))
            sums = ys[spot].astype(F32)
            for d in range(3):
                sums = sums + landing[k][s][(d, *kept_index(place, kept))].astype(F32)
            sums = sums.astype(BF16)
            if s < 2:
                ys[spot] = sums
            else:
                lay_z[start // 32:(start + count) // 32, c] = sums.reshape(count // 32, 32, 128)
            return 0

        if kept:
            lax.fori_loop(0, 4 ** len(kept), add, 0)
        else:
            add(0, 0)

    sums = [[None] * 3 for _ in range(3)]
    for k in range(3):
        sums[k][0] = scatter_stage(k, 0)
    for s in range(3):
        for k in range(3):
            scatter_sum(k, s, sums[k][s])
            if s < 2:
                sums[k][s + 1] = scatter_stage(k, s + 1)

    lay_copy = pltpu.make_async_remote_copy(
        src_ref=lay_z.at[:, c], dst_ref=lay_z.at[:, c], send_sem=fin_s.at[1], recv_sem=fin_r.at[1],
        device_id=sibling, device_id_type=MESH,
    )
    lay_copy.start()
    for k in range(3):
        for s in range(3):
            for copy in stages[k][s]:
                copy.wait_send()
            for copy in sums[k][s]:
                copy.wait_send()

    for copy, z_ref, out in ((res_copy, res_z, res_out), (lay_copy, lay_z, lay_out)):
        copy.wait_send()
        pltpu.make_async_remote_copy(
            src_ref=z_ref.at[:, 1 - c], dst_ref=z_ref.at[:, 1 - c],
            send_sem=fin_s.at[0], recv_sem=fin_r.at[0 if z_ref is res_z else 1],
            device_id=sibling, device_id_type=MESH,
        ).wait_recv()
        ordered = jnp.dot(perm[...], z_ref[...].reshape(512, 128), preferred_element_type=F32)
        ordered = jnp.where(c == 0, ordered, pltpu.roll(ordered, 64, 1))
        out[...] = ordered[:, 0:64].astype(BF16)


def layer(att, gain, slots, resid, out_w, gate_w, up_w, down_w):
    vmem = pl.BlockSpec(memory_space=pltpu.VMEM)
    hbm = pl.BlockSpec(memory_space=pl.ANY)
    dma = pltpu.SemaphoreType.DMA
    landing = []
    for k in range(3):
        for s in range(3):
            shape = (3, *kept_shape(SCATTER_ORDER[k][s + 1:]), SCATTER_ROWS[k][1], 128)
            landing.append(pltpu.VMEM(shape, BF16))
    return pl.pallas_call(
        layer_kernel,
        out_shape=[jax.ShapeDtypeStruct((512, 64), BF16)] * 2,
        in_specs=[vmem, vmem, vmem, hbm, hbm, hbm, hbm, hbm],
        out_specs=[vmem, vmem],
        scratch_shapes=[
            pltpu.VMEM((16, 8, 128), F32),
            pltpu.VMEM((8, 32, 1024), BF16),
            pltpu.VMEM((512, 512), BF16),
            pltpu.VMEM((512, 512), BF16),
            pltpu.VMEM((1024, 512), BF16),
            pltpu.VMEM((1024, 512), BF16),
            pltpu.VMEM((D, HID), BF16),
            pltpu.VMEM((D, HID), BF16),
            pltpu.VMEM((D, HID), BF16),
            pltpu.VMEM((D, HID), BF16),
            pltpu.VMEM((HID, D), BF16),
            pltpu.VMEM((HID, D), BF16),
            pltpu.VMEM((8, 32, 1024), BF16),
            pltpu.VMEM((7, 32, 1024), BF16),
            pltpu.VMEM((2, 4, 2, 4, 32, 1024), BF16),
            pltpu.VMEM((2, 4, 2, 4, 256, 128), BF16),
            pltpu.VMEM((256, HID), F32),
            pltpu.VMEM((256, HID), F32),
            pltpu.VMEM((256, HID), F32),
            pltpu.VMEM((256, HID), F32),
            pltpu.VMEM((256, 128), F32),
            pltpu.VMEM((512, 512), BF16),
            pltpu.VMEM((512, 128), F32),
            pltpu.VMEM((256, HID), BF16),
            pltpu.VMEM((256, HID), BF16),
            pltpu.VMEM((8, 2, 32, 128), BF16),
            pltpu.VMEM((8, 2, 32, 128), BF16),
            pltpu.VMEM((32, 1024), F32),
            *landing,
            dma((5,)),
            dma((5,)), dma((5,)),
            dma((7,)), dma((7,)),
            dma((15,)), dma((15,)),
            dma((7,)), dma((7,)),
            dma((3, 3, 3)), dma((3, 3, 3)),
            dma((3, 3, 3)), dma((3, 3, 3)),
            dma((2,)), dma((2,)),
        ],
        compiler_params=pltpu.CompilerParams(
            collective_id=0, has_side_effects=True, vmem_limit_bytes=56 * 2**20
        ),
        cost_estimate=pl.CostEstimate(flops=6 * 10**9, bytes_accessed=26 * 10**6, transcendentals=0),
        name="layer",
    )(att, gain, slots, resid, out_w, gate_w, up_w, down_w)


def per_device(
    query,
    new_key,
    new_value,
    key_cache,
    value_cache,
    lengths,
    slot_row,
    resid,
    out_weight,
    norm_gain,
    gate_weight,
    up_weight,
    down_weight,
):
    attended = attend_local(query, new_key, new_value, key_cache, value_cache, lengths)
    gain = jnp.pad(norm_gain.astype(F32).reshape(4, 128), ((0, 4), (0, 0)))
    slots = jnp.broadcast_to(slot_row[None, :], (8, 512))
    residual, output = layer(
        attended, gain, slots, resid, out_weight, gate_weight, up_weight, down_weight
    )
    return (residual, output)


def solution(mesh):
    placed = (
        P("grp", "head"),
        P("grp", "head"),
        P("grp", "head"),
        P("grp", "head", None, None),
        P("grp", "head", None, None),
        P("grp"),
        P(),
        P(None, "grp"),
        P("head", "grp"),
        P("grp"),
        P(None, ("grp", "head")),
        P(None, ("grp", "head")),
        P(("grp", "head"), None),
    )
    return jax.shard_map(
        per_device,
        mesh=mesh,
        in_specs=placed,
        out_specs=(P(None, ("grp", "head")), P(None, ("grp", "head"))),
        check_vma=False,
    )
```

```python
import jax
import jax.numpy as jnp
from jax import lax
from jax.experimental import pallas as pl
from jax.experimental.pallas import tpu as pltpu
from jax.sharding import PartitionSpec as P

D = 8192
HD = 128
PER_KV = 8
CTX = 1024
SLOTS = 32
HID = 224
RING = 8
UNROLL = 4
MESH = pl.DeviceIdType.MESH
BF16 = jnp.bfloat16
F32 = jnp.float32
NT = (((1,), (1,)), ((), ()))

GATHER_LANES = ((0, 384), (384, 384), (768, 256))
GATHER_ORDER = ("zxy", "yzx", "xyz")
SCATTER_ROWS = ((0, 96), (96, 96), (192, 64))
SCATTER_ORDER = ("yzx", "zxy", "xyz")
BESIDE = (0, -1, 1, 2)


def device_at(x, y, z, c):
    return ((x // 2) * 8 + y * 2 + c, (x % 2) * 4 + z)


def block_index(where):
    x, y, z = where["x"], where["y"], where["z"]
    if x is None:
        xl, xh = slice(None), slice(None)
    else:
        xl, xh = x % 2, x // 2
    return (xl, slice(None) if z is None else z, xh, slice(None) if y is None else y)


def kept_index(where, kept):
    index = ()
    if "x" in kept:
        index += (where["x"] % 2,)
    if "z" in kept:
        index += (where["z"],)
    if "x" in kept:
        index += (where["x"] // 2,)
    if "y" in kept:
        index += (where["y"],)
    return index


def kept_shape(kept):
    shape = ()
    if "x" in kept:
        shape += (2,)
    if "z" in kept:
        shape += (4,)
    if "x" in kept:
        shape += (2,)
    if "y" in kept:
        shape += (4,)
    return shape


def layer_kernel(
    query, new_key, new_value, lengths, gain, slots, keys, values, resid, out_w, gate_w, up_w, down_w,
    res_out, lay_out,
    key_ring, value_ring, heads, mixed, new_key_f, new_value_f,
    gain_own, gains, got_att, resid_own, resid_sib, ow_own, ow_sib,
    gate_up, down_all,
    proj, proj_got, xs, ys, acc, square,
    perm, slot_col, hidden, res_z, lay_z, res_rows,
    *rest,
):
    landing = [[rest[k * 3 + s] for s in range(3)] for k in range(3)]
    transit = [[rest[9 + k * 3 + s] for s in range(3)] for k in range(3)]
    (kv_sem, load_sem, swap_s, swap_r, att_s, att_r, gain_s, gain_r, proj_s, proj_r,
     ga_s, ga_r, sc_s, sc_r, fin_s, fin_r) = rest[18:]

    g = lax.axis_index("grp")
    h = lax.axis_index("head")
    xh, y, c = g // 8, (g // 2) % 4, g % 2
    xl, z = h // 4, h % 4
    me = {"x": xh * 2 + xl, "y": y, "z": z}

    def on_axis(axis, step):
        place = dict(me)
        place[axis] = (me[axis] + step + 4) % 4
        return place

    def at(place, core):
        return device_at(place["x"], place["y"], place["z"], core)

    sibling = at(me, 1 - c)
    barrier = pltpu.get_barrier_semaphore()
    partners = []
    for i in range(1, 16):
        partners.append(((g + i) % 16, h))
    for i in range(1, 8):
        partners.append((g, (h + i) % 8))
    partners.append(((g + 8) % 16, (h + 4) % 8))
    for partner in partners:
        pl.semaphore_signal(barrier, inc=1, device_id=partner, device_id_type=MESH)

    def cache_copies(row, ring):
        return (
            pltpu.make_async_copy(keys.at[row, 0], key_ring.at[ring], kv_sem.at[0, ring]),
            pltpu.make_async_copy(values.at[row, 0], value_ring.at[ring], kv_sem.at[1, ring]),
        )

    for row in range(RING):
        for copy in cache_copies(row, row):
            copy.start()
    new_key_f[...] = new_key[...].astype(F32)
    new_value_f[...] = new_value[...].astype(F32)
    for j in range(PER_KV):
        heads[:, j, :] = query[:, j * HD:(j + 1) * HD].astype(F32)
    for t in range(4):
        gain_own[t:t + 1, :] = gain[:, t * 128:(t + 1) * 128].astype(F32)
    gain_own[4:8, :] = jnp.zeros((4, 128), F32)
    pl.semaphore_wait(barrier, len(partners))

    swaps = []
    for i, (src, dst) in enumerate(
        ((out_w, ow_sib), (resid, resid_sib), (gate_w, gate_up.at[pl.ds(HID, HID)]),
         (up_w, gate_up.at[pl.ds(3 * HID, HID)]), (down_w, down_all.at[pl.ds(HID, HID)]))
    ):
        copy = pltpu.make_async_remote_copy(
            src_ref=src, dst_ref=dst, send_sem=swap_s.at[i], recv_sem=swap_r.at[i],
            device_id=sibling, device_id_type=MESH,
        )
        copy.start()
        swaps.append(copy)
    gain_copies = []
    for i in range(1, 16):
        copy = pltpu.make_async_remote_copy(
            src_ref=gain_own,
            dst_ref=gains.at[g],
            send_sem=gain_s.at[i - 1],
            recv_sem=gain_r.at[i - 1],
            device_id=((g + i) % 16, h),
            device_id_type=MESH,
        )
        copy.start()
        gain_copies.append(copy)
    gains[g] = gain_own[...]

    spot_lane = lax.broadcasted_iota(jnp.int32, (PER_KV, CTX), 1)

    def attend(step, _):
        for u in range(UNROLL):
            row = step * UNROLL + u
            ring = row % RING
            for copy in cache_copies(row, ring):
                copy.wait()
        for u in range(UNROLL):
            row = step * UNROLL + u
            ring = row % RING
            head = heads[row]
            scores = lax.dot_general(
                head.astype(BF16), key_ring[ring], NT, preferred_element_type=F32
            ) * HD ** (-0.5)
            own = jnp.sum(head * new_key_f[pl.ds(row, 1), :], axis=1, keepdims=True) * HD ** (-0.5)
            live = spot_lane < lengths[row]
            scores = jnp.where(live, scores, -1e30)
            top = jnp.maximum(jnp.max(scores, axis=1, keepdims=True), own)
            weights = jnp.where(live, jnp.exp(scores - top), 0.0)
            own = jnp.exp(own - top)
            share = 1.0 / (jnp.sum(weights, axis=1, keepdims=True) + own)
            weights = (weights * share).astype(BF16)
            own = (own * share).astype(BF16).astype(F32)
            result = jnp.dot(weights, value_ring[ring], preferred_element_type=F32)
            mixed[row] = result + own * new_value_f[pl.ds(row, 1), :]
        for u in range(UNROLL):
            row = step * UNROLL + u
            ring = row % RING

            @pl.when(row + RING < SLOTS)
            def _():
                for copy in cache_copies(row + RING, ring):
                    copy.start()
        return 0

    att_copies = []
    half = SLOTS // 2
    for part in range(2):
        steps = half // UNROLL
        lax.fori_loop(part * steps, (part + 1) * steps, attend, 0)
        rows = pl.ds(part * half, half)
        for j in range(PER_KV):
            got_att[xh * 4 + y, rows, j * HD:(j + 1) * HD] = mixed[rows, j, :].astype(BF16)
        for i in (6, 5, 4, 2, 7, 3, 1):
            xy = ((xh + i // 4) % 2) * 4 + (y + i) % 4
            copy = pltpu.make_async_remote_copy(
                src_ref=got_att.at[xh * 4 + y, rows],
                dst_ref=got_att.at[xh * 4 + y, rows],
                send_sem=att_s.at[part, i - 1],
                recv_sem=att_r.at[part, i - 1],
                device_id=((xy // 4) * 8 + (xy % 4) * 2 + c, h),
                device_id_type=MESH,
            )
            copy.start()
            att_copies.append((i, copy))
    loads = []
    for i, (src, dst) in enumerate(
        ((out_w, ow_own), (resid, resid_own), (gate_w, gate_up.at[pl.ds(0, HID)]),
         (up_w, gate_up.at[pl.ds(2 * HID, HID)]), (down_w, down_all.at[pl.ds(0, HID)]))
    ):
        copy = pltpu.make_async_copy(src, dst, load_sem.at[i])
        copy.start()
        loads.append(copy)

    slot_line = slots[...]
    for t in range(4):
        tile = jnp.broadcast_to(slot_line[:, t * 128:(t + 1) * 128].astype(F32), (128, 128))
        slot_col[t * 128:(t + 1) * 128, :] = tile.T
        batch = lax.broadcasted_iota(jnp.int32, (128, 512), 0) + t * 128
        perm[t * 128:(t + 1) * 128, :] = jnp.where(batch == slot_line, 1.0, 0.0).astype(BF16)
    square[...] = jnp.zeros_like(square)
    acc[...] = jnp.zeros_like(acc)

    loads[1].wait()
    swaps[1].wait()
    my_slots = slot_col[pl.ds(pl.multiple_of((2 * h + c) * 32, 32), 32), :]
    lane = lax.broadcasted_iota(jnp.int32, (32, 128), 1).astype(F32)
    pick = jnp.concatenate(
        [jnp.where(my_slots == lane + 128.0 * t, 1.0, 0.0).astype(BF16) for t in range(4)], axis=1
    )

    @pl.when(c == 0)
    def _():
        res_rows[:, 0:512] = jnp.dot(pick, resid_own[...], preferred_element_type=F32)
        res_rows[:, 512:1024] = jnp.dot(pick, resid_sib[...], preferred_element_type=F32)

    @pl.when(c == 1)
    def _():
        res_rows[:, 0:512] = jnp.dot(pick, resid_sib[...], preferred_element_type=F32)
        res_rows[:, 512:1024] = jnp.dot(pick, resid_own[...], preferred_element_type=F32)

    loads[0].wait()
    swaps[0].wait()
    for side in range(2):
        for i, copy in att_copies:
            if (i < 4) == (side == 0):
                copy.wait()
        xx = (xh + side) % 2
        part = got_att[pl.ds(xx * 4, 4)].reshape(128, 1024)
        own_part = jnp.dot(part, ow_own[...], preferred_element_type=F32).astype(BF16)
        sib_part = jnp.dot(part, ow_sib[...], preferred_element_type=F32).astype(BF16)
        proj[pl.ds(xx * 4, 4), :, pl.ds(pl.multiple_of(c * 512, 512), 512)] = own_part.reshape(4, 32, 512)
        proj[pl.ds(xx * 4, 4), :, pl.ds(pl.multiple_of((1 - c) * 512, 512), 512)] = sib_part.reshape(
            4, 32, 512
        )
        for k in range(3):
            lanes = pl.ds(*GATHER_LANES[k])
            for j in range(4):
                head = xx * 4 + (z + 2 + j) % 4

                @pl.when(head != h)
                def _():
                    pltpu.make_async_remote_copy(
                        src_ref=proj.at[head, :, lanes],
                        dst_ref=proj_got.at[h, :, lanes],
                        send_sem=proj_s.at[k, head],
                        recv_sem=proj_r.at[k, h],
                        device_id=(g, head),
                        device_id_type=MESH,
                    ).start()

    def proj_copy(k, head):
        lanes = pl.ds(*GATHER_LANES[k])
        return pltpu.make_async_remote_copy(
            src_ref=proj.at[head, :, lanes],
            dst_ref=proj_got.at[head, :, lanes],
            send_sem=proj_s.at[k, head],
            recv_sem=proj_r.at[k, head],
            device_id=(g, head),
            device_id_type=MESH,
        )

    gathers = {}

    def gather_spot(k, s, q, shift):
        order = GATHER_ORDER[k]
        place = dict(me)
        for a in order[:s]:
            place[a] = None
        if s == 2:
            place[order[1]] = (me[order[1]] + BESIDE[q] + 4) % 4
        place[order[s]] = (me[order[s]] + shift + 4) % 4
        return place

    def gather_copy(k, s, q, which):
        shift, rows, step = (
            (0, pl.ds(0, 32), 1), (0, pl.ds(0, 32), -1), (-1, pl.ds(0, 16), 1), (1, pl.ds(16, 16), -1)
        )[which]
        region = xs.at[(*block_index(gather_spot(k, s, q, shift)), rows, pl.ds(*GATHER_LANES[k]))]
        index = 4 * (s + q) + which
        copy = pltpu.make_async_remote_copy(
            src_ref=region, dst_ref=region, send_sem=ga_s.at[k, index], recv_sem=ga_r.at[k, index],
            device_id=at(on_axis(GATHER_ORDER[k][s], step), c), device_id_type=MESH,
        )
        copy.start()
        gathers[k, s, q, which] = copy

    def direct(k, s, q):
        gather_copy(k, s, q, 0)
        gather_copy(k, s, q, 1)

    def forward(k, s, q):
        gathers[k, s, q, 0].wait_recv()
        gather_copy(k, s, q, 2)
        gathers[k, s, q, 1].wait_recv()
        gather_copy(k, s, q, 3)

    def finish(k, s, q):
        gathers[k, s, q, 2].wait_recv()
        gathers[k, s, q, 3].wait_recv()

    mine = block_index(me)
    for k in range(3):
        lanes = pl.ds(*GATHER_LANES[k])
        total = res_rows[:, lanes] + proj[h, :, lanes].astype(F32)
        for i in range(1, 8):
            head = (h + i) % 8
            proj_copy(k, head).wait_recv()
            total = total + proj_got[head, :, lanes].astype(F32)
        xs[(*mine, slice(None), lanes)] = total.astype(BF16)
        direct(k, 0, 0)
    for k in range(3):
        forward(k, 0, 0)
    for k in range(3):
        finish(k, 0, 0)
        direct(k, 1, 0)
        direct(k, 2, 0)
    for k in range(3):
        forward(k, 1, 0)
        direct(k, 2, 1)
        direct(k, 2, 2)
    for k in range(3):
        finish(k, 1, 0)
        direct(k, 2, 3)

    def feed(k, blocks):
        start, width = GATHER_LANES[k]
        total = None
        sums = square[...]
        for bxh, by in blocks:
            block = bxh * 4 + by
            pieces = []
            for t in range(start // 128, (start + width) // 128):
                part = xs[:, :, bxh, by, :, t * 128:(t + 1) * 128].reshape(256, 128).astype(F32)
                sums = sums + part * part
                scale = gains[2 * block + t // 4, t % 4:t % 4 + 1, :]
                pieces.append((part * scale).astype(BF16))
            scaled = jnp.concatenate(pieces, axis=1)
            depth = pl.ds(pl.multiple_of(block * 1024 + start, 128), width)
            term = lax.dot_general(gate_up[:, depth], scaled, NT, preferred_element_type=F32)
            total = term if total is None else total + term
        square[...] = sums
        acc[...] += total

    def feed_y(k, by):
        feed(k, ((0, by), (1, by)))

    def feed_x(k, bxh):
        def pair(i, _):
            feed(k, ((bxh, 2 * i), (bxh, 2 * i + 1)))
            return 0

        lax.fori_loop(0, 2, pair, 0)

    def feed_all(k):
        def pair(i, _):
            feed(k, ((0, i), (1, i)))
            return 0

        lax.fori_loop(0, 4, pair, 0)

    for copy in gain_copies:
        copy.wait()
    for i in (2, 3):
        loads[i].wait()
        swaps[i].wait()
    feed_y(0, y)
    for q in range(4):
        for k in (2, 0, 1):
            forward(k, 2, q)
    feed_y(0, (y + 1) % 4)
    feed_y(0, (y + 3) % 4)
    feed_x(1, xh)
    for q in range(4):
        finish(2, 2, q)
    feed_all(2)
    for q in range(4):
        finish(0, 2, q)
    feed_y(0, (y + 2) % 4)
    for q in range(4):
        finish(1, 2, q)
    feed_x(1, 1 - xh)

    norm = lax.rsqrt(jnp.sum(square[...].T, axis=0, keepdims=True) / D + 1e-05)
    gate = acc[0:2 * HID, :] * norm
    up = acc[2 * HID:4 * HID, :] * norm
    hidden[...] = (gate * jax.nn.sigmoid(gate) * up).T.astype(BF16)

    lane_low = lax.broadcasted_iota(jnp.int32, (256, 128), 1) < 64
    odd = h % 2
    tiles = []
    for core in range(2):
        window = pl.ds(pl.multiple_of(core * 512 + (h // 2) * 128, 128), 128)
        tiles.append(xs[:, :, xh, y, :, window].reshape(256, 128).astype(F32))
    even_pack = jnp.where(lane_low, tiles[0], pltpu.roll(tiles[1], 64, 1))
    odd_pack = jnp.where(lane_low, pltpu.roll(tiles[0], 64, 1), tiles[1])
    packed = jnp.where(odd == 0, even_pack, odd_pack)
    res_z[:, c] = packed.astype(BF16).reshape(8, 32, 128)
    res_copy = pltpu.make_async_remote_copy(
        src_ref=res_z.at[:, c], dst_ref=res_z.at[:, c], send_sem=fin_s.at[0], recv_sem=fin_r.at[0],
        device_id=sibling, device_id_type=MESH,
    )
    res_copy.start()

    loads[4].wait()
    swaps[4].wait()

    def project(block, _):
        bxh, by = block // 4, block % 4
        col = pl.ds(pl.multiple_of(block * 1024, 1024), 1024)
        wide = jnp.dot(hidden[...], down_all[:, col], preferred_element_type=F32)
        for pair in range(4):
            low = wide[:, pair * 128:(pair + 1) * 128]
            high = wide[:, 512 + pair * 128:512 + (pair + 1) * 128]
            first = jnp.where(lane_low, low, pltpu.roll(high, 64, 1)).astype(BF16)
            second = jnp.where(lane_low, pltpu.roll(low, 64, 1), high).astype(BF16)
            ys[pair // 2, (pair % 2) * 2, bxh, by] = first
            ys[pair // 2, (pair % 2) * 2 + 1, bxh, by] = second
        return 0

    lax.fori_loop(0, 8, project, 0)

    scatters = {}

    def halves(k):
        start, count = SCATTER_ROWS[k]
        return ((start, count // 2), (start + count // 2, count // 2))

    def scatter_place(k, s, shift):
        order = SCATTER_ORDER[k]
        place = dict(me)
        place[order[s]] = (me[order[s]] + shift + 4) % 4
        for a in order[s + 1:]:
            place[a] = None
        return place

    def scatter_copy(k, s, which):
        target, part, step = ((2, 0, 1), (2, 1, -1), (1, 1, 1), (-1, 0, -1), (1, 0, 1), (-1, 1, -1))[which]
        start, count = halves(k)[part]
        if which < 2:
            dst = transit[k][s].at[which]
        else:
            side = 0 if step == 1 else 1
            everything = (slice(None),) * len(kept_shape(SCATTER_ORDER[k][s + 1:]))
            dst = landing[k][s].at[(side, *everything, pl.ds(start - SCATTER_ROWS[k][0], count))]
        copy = pltpu.make_async_remote_copy(
            src_ref=ys.at[(*block_index(scatter_place(k, s, target)), pl.ds(start, count))],
            dst_ref=dst, send_sem=sc_s.at[k, s, which], recv_sem=sc_r.at[k, s, which],
            device_id=at(on_axis(SCATTER_ORDER[k][s], step), c), device_id_type=MESH,
        )
        copy.start()
        scatters[k, s, which] = copy

    def each_block(k, s, shift, body):
        kept = SCATTER_ORDER[k][s + 1:]

        def one(block, _):
            place = scatter_place(k, s, shift)
            for i, a in enumerate(kept):
                place[a] = (block // 4**i) % 4
            body(block_index(place), kept_index(place, kept))
            return 0

        if kept:
            lax.fori_loop(0, 4 ** len(kept), one, 0)
        else:
            one(0, 0)

    def scatter_begin(k, s):
        for which in range(4):
            scatter_copy(k, s, which)

    def scatter_pass(k, s):
        for which, shift in ((0, 1), (1, -1)):
            scatters[k, s, which].wait_recv()
            rows = pl.ds(*halves(k)[which])

            def add(spot, kept_spot, which=which, rows=rows):
                both = ys[(*spot, rows)].astype(F32) + transit[k][s][(which, *kept_spot)].astype(F32)
                ys[(*spot, rows)] = both.astype(BF16)

            each_block(k, s, shift, add)
            scatter_copy(k, s, 4 + which)

    def scatter_end(k, s):
        for which in range(2, 6):
            scatters[k, s, which].wait_recv()
        start, count = SCATTER_ROWS[k]
        rows = pl.ds(start, count)

        def add(spot, kept_spot):
            sums = ys[(*spot, rows)].astype(F32)
            for side in range(2):
                sums = sums + landing[k][s][(side, *kept_spot)].astype(F32)
            sums = sums.astype(BF16)
            if s < 2:
                ys[(*spot, rows)] = sums
            else:
                lay_z[start // 32:(start + count) // 32, c] = sums.reshape(count // 32, 32, 128)

        each_block(k, s, 0, add)

    for k in range(3):
        scatter_begin(k, 0)
    for s in range(3):
        for k in range(3):
            scatter_pass(k, s)
        for k in range(3):
            scatter_end(k, s)
            if s < 2:
                scatter_begin(k, s + 1)

    lay_copy = pltpu.make_async_remote_copy(
        src_ref=lay_z.at[:, c], dst_ref=lay_z.at[:, c], send_sem=fin_s.at[1], recv_sem=fin_r.at[1],
        device_id=sibling, device_id_type=MESH,
    )
    lay_copy.start()
    for k in range(3):
        for i in range(1, 8):
            proj_copy(k, (h + i) % 8).wait_send()
    for copy in gathers.values():
        copy.wait_send()
    for copy in scatters.values():
        copy.wait_send()

    for i, (copy, z_ref, out) in enumerate(((res_copy, res_z, res_out), (lay_copy, lay_z, lay_out))):
        copy.wait_send()
        pltpu.make_async_remote_copy(
            src_ref=z_ref.at[:, 1 - c], dst_ref=z_ref.at[:, 1 - c],
            send_sem=fin_s.at[i], recv_sem=fin_r.at[i],
            device_id=sibling, device_id_type=MESH,
        ).wait_recv()
        ordered = jnp.dot(perm[...], z_ref[...].reshape(512, 128), preferred_element_type=F32)
        ordered = jnp.where(c == 0, ordered, pltpu.roll(ordered, 64, 1))
        out[...] = ordered.T[0:64, :].astype(BF16)


def layer(query, new_key, new_value, lengths, gain, slots, *hbm_args):
    vmem = pl.BlockSpec(memory_space=pltpu.VMEM)
    smem = pl.BlockSpec(memory_space=pltpu.SMEM)
    hbm = pl.BlockSpec(memory_space=pl.ANY)
    dma = pltpu.SemaphoreType.DMA
    landing, transit = [], []
    for k in range(3):
        for s in range(3):
            kept, count = kept_shape(SCATTER_ORDER[k][s + 1:]), SCATTER_ROWS[k][1]
            landing.append(pltpu.VMEM((2, *kept, count, 128), BF16))
            transit.append(pltpu.VMEM((2, *kept, count // 2, 128), BF16))
    return pl.pallas_call(
        layer_kernel,
        out_shape=[jax.ShapeDtypeStruct((64, 512), BF16)] * 2,
        in_specs=[vmem, vmem, vmem, smem, vmem, vmem] + [hbm] * len(hbm_args),
        out_specs=[vmem, vmem],
        scratch_shapes=[
            pltpu.VMEM((RING, CTX, HD), BF16),
            pltpu.VMEM((RING, CTX, HD), BF16),
            pltpu.VMEM((SLOTS, PER_KV, HD), F32),
            pltpu.VMEM((SLOTS, PER_KV, HD), F32),
            pltpu.VMEM((SLOTS, HD), F32),
            pltpu.VMEM((SLOTS, HD), F32),
            pltpu.VMEM((8, 128), F32),
            pltpu.VMEM((16, 8, 128), F32),
            pltpu.VMEM((8, 32, 1024), BF16),
            pltpu.VMEM((512, 512), BF16),
            pltpu.VMEM((512, 512), BF16),
            pltpu.VMEM((1024, 512), BF16),
            pltpu.VMEM((1024, 512), BF16),
            pltpu.VMEM((4 * HID, D), BF16),
            pltpu.VMEM((2 * HID, D), BF16),
            pltpu.VMEM((8, 32, 1024), BF16),
            pltpu.VMEM((8, 32, 1024), BF16),
            pltpu.VMEM((2, 4, 2, 4, 32, 1024), BF16),
            pltpu.VMEM((2, 4, 2, 4, 256, 128), BF16),
            pltpu.VMEM((4 * HID, 256), F32),
            pltpu.VMEM((256, 128), F32),
            pltpu.VMEM((512, 512), BF16),
            pltpu.VMEM((512, 128), F32),
            pltpu.VMEM((256, 2 * HID), BF16),
            pltpu.VMEM((8, 2, 32, 128), BF16),
            pltpu.VMEM((8, 2, 32, 128), BF16),
            pltpu.VMEM((32, 1024), F32),
            *landing,
            *transit,
            dma((2, RING)),
            dma((5,)),
            dma((5,)), dma((5,)),
            dma((2, 7)), dma((2, 7)),
            dma((15,)), dma((15,)),
            dma((3, 8)), dma((3, 8)),
            dma((3, 24)), dma((3, 24)),
            dma((3, 3, 6)), dma((3, 3, 6)),
            dma((2,)), dma((2,)),
        ],
        compiler_params=pltpu.CompilerParams(
            collective_id=0, has_side_effects=True, vmem_limit_bytes=58 * 2**20
        ),
        cost_estimate=pl.CostEstimate(flops=6 * 10**9, bytes_accessed=42 * 10**6, transcendentals=0),
        name="layer",
    )(query, new_key, new_value, lengths, gain, slots, *hbm_args)


def per_device(
    query,
    new_key,
    new_value,
    key_cache,
    value_cache,
    lengths,
    slot_row,
    resid,
    out_weight,
    norm_gain,
    gate_weight,
    up_weight,
    down_weight,
):
    residual, output = layer(
        query, new_key, new_value, lengths, norm_gain[None, :], slot_row[None, :],
        key_cache, value_cache, resid, out_weight, gate_weight.T, up_weight.T, down_weight,
    )
    return (residual.T, output.T)


def solution(mesh):
    placed = (
        P("grp", "head"),
        P("grp", "head"),
        P("grp", "head"),
        P("grp", "head", None, None),
        P("grp", "head", None, None),
        P("grp"),
        P(),
        P(None, "grp"),
        P("head", "grp"),
        P("grp"),
        P(None, ("grp", "head")),
        P(None, ("grp", "head")),
        P(("grp", "head"), None),
    )
    return jax.shard_map(
        per_device,
        mesh=mesh,
        in_specs=placed,
        out_specs=(P(None, ("grp", "head")), P(None, ("grp", "head"))),
        check_vma=False,
    )
```

```python
import jax
import jax.numpy as jnp
from jax import lax
from jax.experimental import pallas as pl
from jax.experimental.pallas import tpu as pltpu
from jax.sharding import PartitionSpec as P

D = 8192
HD = 128
PER_KV = 8
CTX = 1024
SLOTS = 32
HID = 224
RING = 8
UNROLL = 4
MESH = pl.DeviceIdType.MESH
BF16 = jnp.bfloat16
F32 = jnp.float32
NT = (((1,), (1,)), ((), ()))

GATHER_LANES = ((0, 384), (384, 384), (768, 256))
GATHER_ORDER = ("xzy", "yzx", "xyz")
SCATTER_ROWS = ((0, 96), (96, 96), (192, 64))
SCATTER_ORDER = ("zyx", "xyz", "yzx")
BESIDE = (0, -1, 1, 2)
GROUPS = (2, -1, 1, 0)


def device_at(x, y, z, c):
    return ((x // 2) * 8 + y * 2 + c, (x % 2) * 4 + z)


def block_index(where):
    x, y, z = where["x"], where["y"], where["z"]
    if x is None:
        xl, xh = slice(None), slice(None)
    else:
        xl, xh = x % 2, x // 2
    return (xl, slice(None) if z is None else z, xh, slice(None) if y is None else y)


def kept_index(where, kept):
    index = ()
    if "x" in kept:
        index += (where["x"] % 2,)
    if "z" in kept:
        index += (where["z"],)
    if "x" in kept:
        index += (where["x"] // 2,)
    if "y" in kept:
        index += (where["y"],)
    return index


def kept_block(where, kept):
    index = ()
    if "x" in kept:
        index += (slice(None) if where["x"] is None else where["x"] % 2,)
    if "z" in kept:
        index += (slice(None) if where["z"] is None else where["z"],)
    if "x" in kept:
        index += (slice(None) if where["x"] is None else where["x"] // 2,)
    if "y" in kept:
        index += (slice(None) if where["y"] is None else where["y"],)
    return index


def kept_shape(kept):
    shape = ()
    if "x" in kept:
        shape += (2,)
    if "z" in kept:
        shape += (4,)
    if "x" in kept:
        shape += (2,)
    if "y" in kept:
        shape += (4,)
    return shape


def layer_kernel(
    query, new_key, new_value, lengths, gain, slots, keys, values, resid, out_w, gate_w, up_w, down_w,
    res_out, lay_out,
    key_ring, value_ring, heads, mixed, new_key_f, new_value_f,
    gain_own, gains, got_att, resid_own, resid_sib, ow_own, ow_sib,
    gate_up, down_all,
    proj, proj_got, xs, ys, acc, square,
    perm, slot_col, hidden, res_z, lay_z, res_rows,
    *rest,
):
    landing = [[rest[k * 3 + s] for s in range(3)] for k in range(3)]
    transit = [[rest[9 + k * 2 + s] for s in range(2)] for k in range(3)]
    (kv_sem, load_sem, swap_s, swap_r, att_s, att_r, gain_s, gain_r, proj_s, proj_r,
     ga_s, ga_r, sc_s, sc_r, fin_s, fin_r) = rest[15:]

    g = lax.axis_index("grp")
    h = lax.axis_index("head")
    xh, y, c = g // 8, (g // 2) % 4, g % 2
    xl, z = h // 4, h % 4
    me = {"x": xh * 2 + xl, "y": y, "z": z}

    def on_axis(axis, step):
        place = dict(me)
        place[axis] = (me[axis] + step + 4) % 4
        return place

    def at(place, core):
        return device_at(place["x"], place["y"], place["z"], core)

    sibling = at(me, 1 - c)
    barrier = pltpu.get_barrier_semaphore()
    partners = []
    for i in range(1, 16):
        partners.append(((g + i) % 16, h))
    for i in range(1, 8):
        partners.append((g, (h + i) % 8))
    partners.append(((g + 8) % 16, (h + 4) % 8))
    for partner in partners:
        pl.semaphore_signal(barrier, inc=1, device_id=partner, device_id_type=MESH)

    def cache_copies(row, ring):
        return (
            pltpu.make_async_copy(keys.at[row, 0], key_ring.at[ring], kv_sem.at[0, ring]),
            pltpu.make_async_copy(values.at[row, 0], value_ring.at[ring], kv_sem.at[1, ring]),
        )

    for row in range(RING):
        for copy in cache_copies(row, row):
            copy.start()
    new_key_f[...] = new_key[...].astype(F32)
    new_value_f[...] = new_value[...].astype(F32)
    for j in range(PER_KV):
        heads[:, j, :] = query[:, j * HD:(j + 1) * HD].astype(F32)
    for t in range(4):
        gain_own[t:t + 1, :] = gain[:, t * 128:(t + 1) * 128].astype(F32)
    gain_own[4:8, :] = jnp.zeros((4, 128), F32)
    spot_lane = lax.broadcasted_iota(jnp.int32, (PER_KV, CTX), 1)

    def attend(step, _):
        for u in range(UNROLL):
            row = step * UNROLL + u
            ring = row % RING
            for copy in cache_copies(row, ring):
                copy.wait()
        group = [step * UNROLL + u for u in range(UNROLL)]
        query_rows = [heads[row] for row in group]
        scores = [
            lax.dot_general(
                head.astype(BF16), key_ring[row % RING], NT, preferred_element_type=F32
            ) * HD ** (-0.5)
            for row, head in zip(group, query_rows)
        ]
        own = [
            jnp.sum(head * new_key_f[pl.ds(row, 1), :], axis=1, keepdims=True) * HD ** (-0.5)
            for row, head in zip(group, query_rows)
        ]
        scores = [
            jnp.where(spot_lane < lengths[row], part, -1e30) for row, part in zip(group, scores)
        ]
        tops = [
            jnp.maximum(jnp.max(part, axis=1, keepdims=True), alone) for part, alone in zip(scores, own)
        ]
        weights = [jnp.exp(part - top) for part, top in zip(scores, tops)]
        own = [jnp.exp(alone - top) for alone, top in zip(own, tops)]
        shares = [
            1.0 / (jnp.sum(part, axis=1, keepdims=True) + alone) for part, alone in zip(weights, own)
        ]
        results = [
            jnp.dot((part * share).astype(BF16), value_ring[row % RING], preferred_element_type=F32)
            + (alone * share).astype(BF16).astype(F32) * new_value_f[pl.ds(row, 1), :]
            for row, part, alone, share in zip(group, weights, own, shares)
        ]
        for row, result in zip(group, results):
            mixed[row] = result
        for u in range(UNROLL):
            row = step * UNROLL + u
            ring = row % RING

            @pl.when(row + RING < SLOTS)
            def _():
                for copy in cache_copies(row + RING, ring):
                    copy.start()
        return 0

    swap_list = (
        (out_w, ow_sib), (resid, resid_sib), (gate_w, gate_up.at[pl.ds(HID, HID)]),
        (up_w, gate_up.at[pl.ds(3 * HID, HID)]), (down_w, down_all.at[pl.ds(HID, HID)]),
    )
    swaps = []

    def swap(i):
        copy = pltpu.make_async_remote_copy(
            src_ref=swap_list[i][0], dst_ref=swap_list[i][1], send_sem=swap_s.at[i], recv_sem=swap_r.at[i],
            device_id=sibling, device_id_type=MESH,
        )
        copy.start()
        swaps.append(copy)

    att_copies = []
    half = SLOTS // 2
    for part in range(2):
        steps = half // UNROLL
        lax.fori_loop(part * steps, (part + 1) * steps, attend, 0)
        if part == 0:
            pl.semaphore_wait(barrier, len(partners))
        rows = pl.ds(part * half, half)
        for j in range(PER_KV):
            got_att[xh * 4 + y, rows, j * HD:(j + 1) * HD] = mixed[rows, j, :].astype(BF16)
        for i in (6, 5, 4, 2, 7, 3, 1):
            xy = ((xh + i // 4) % 2) * 4 + (y + i) % 4
            copy = pltpu.make_async_remote_copy(
                src_ref=got_att.at[xh * 4 + y, rows],
                dst_ref=got_att.at[xh * 4 + y, rows],
                send_sem=att_s.at[part, i - 1],
                recv_sem=att_r.at[part, i - 1],
                device_id=((xy // 4) * 8 + (xy % 4) * 2 + c, h),
                device_id_type=MESH,
            )
            copy.start()
            att_copies.append((i, copy))
        if part == 0:
            swap(0)
            swap(1)
    for i in range(2, 5):
        swap(i)
    gain_copies = []
    for i in range(1, 16):
        copy = pltpu.make_async_remote_copy(
            src_ref=gain_own,
            dst_ref=gains.at[g],
            send_sem=gain_s.at[i - 1],
            recv_sem=gain_r.at[i - 1],
            device_id=((g + i) % 16, h),
            device_id_type=MESH,
        )
        copy.start()
        gain_copies.append(copy)
    gains[g] = gain_own[...]
    loads = []
    for i, (src, dst) in enumerate(
        ((out_w, ow_own), (resid, resid_own), (gate_w, gate_up.at[pl.ds(0, HID)]),
         (up_w, gate_up.at[pl.ds(2 * HID, HID)]), (down_w, down_all.at[pl.ds(0, HID)]))
    ):
        copy = pltpu.make_async_copy(src, dst, load_sem.at[i])
        copy.start()
        loads.append(copy)

    slot_line = slots[...]
    for t in range(4):
        tile = jnp.broadcast_to(slot_line[:, t * 128:(t + 1) * 128].astype(F32), (128, 128))
        slot_col[t * 128:(t + 1) * 128, :] = tile.T
        batch = lax.broadcasted_iota(jnp.int32, (128, 512), 0) + t * 128
        perm[t * 128:(t + 1) * 128, :] = jnp.where(batch == slot_line, 1.0, 0.0).astype(BF16)
    square[...] = jnp.zeros_like(square)
    acc[...] = jnp.zeros_like(acc)

    loads[1].wait()
    swaps[1].wait()
    my_slots = slot_col[pl.ds(pl.multiple_of((2 * h + c) * 32, 32), 32), :]
    lane = lax.broadcasted_iota(jnp.int32, (32, 128), 1).astype(F32)
    pick = jnp.concatenate(
        [jnp.where(my_slots == lane + 128.0 * t, 1.0, 0.0).astype(BF16) for t in range(4)], axis=1
    )

    @pl.when(c == 0)
    def _():
        res_rows[:, 0:512] = jnp.dot(pick, resid_own[...], preferred_element_type=F32)
        res_rows[:, 512:1024] = jnp.dot(pick, resid_sib[...], preferred_element_type=F32)

    @pl.when(c == 1)
    def _():
        res_rows[:, 0:512] = jnp.dot(pick, resid_sib[...], preferred_element_type=F32)
        res_rows[:, 512:1024] = jnp.dot(pick, resid_own[...], preferred_element_type=F32)

    loads[0].wait()
    swaps[0].wait()
    for side in range(2):
        for i, copy in att_copies:
            if (i < 4) == (side == 0):
                copy.wait()
        xx = (xh + side) % 2
        part = got_att[pl.ds(xx * 4, 4)].reshape(128, 1024)
        own_part = jnp.dot(part, ow_own[...], preferred_element_type=F32).astype(BF16)
        sib_part = jnp.dot(part, ow_sib[...], preferred_element_type=F32).astype(BF16)
        proj[pl.ds(xx * 4, 4), :, pl.ds(pl.multiple_of(c * 512, 512), 512)] = own_part.reshape(4, 32, 512)
        proj[pl.ds(xx * 4, 4), :, pl.ds(pl.multiple_of((1 - c) * 512, 512), 512)] = sib_part.reshape(
            4, 32, 512
        )
        for k in range(3):
            lanes = pl.ds(*GATHER_LANES[k])
            for j in range(4):
                head = xx * 4 + (z + 2 + j) % 4

                @pl.when(head != h)
                def _():
                    pltpu.make_async_remote_copy(
                        src_ref=proj.at[head, :, lanes],
                        dst_ref=proj_got.at[h, :, lanes],
                        send_sem=proj_s.at[k, head],
                        recv_sem=proj_r.at[k, h],
                        device_id=(g, head),
                        device_id_type=MESH,
                    ).start()

    def proj_copy(k, head):
        lanes = pl.ds(*GATHER_LANES[k])
        return pltpu.make_async_remote_copy(
            src_ref=proj.at[head, :, lanes],
            dst_ref=proj_got.at[head, :, lanes],
            send_sem=proj_s.at[k, head],
            recv_sem=proj_r.at[k, head],
            device_id=(g, head),
            device_id_type=MESH,
        )

    gathers = {}

    def gather_spot(k, s, q, shift):
        order = GATHER_ORDER[k]
        place = dict(me)
        for a in order[:s]:
            place[a] = None
        if s == 2:
            place[order[1]] = (me[order[1]] + BESIDE[q] + 4) % 4
        place[order[s]] = (me[order[s]] + shift + 4) % 4
        return place

    def gather_copy(k, s, q, which):
        shift, rows, step = (
            (0, pl.ds(0, 32), 1), (0, pl.ds(0, 32), -1), (-1, pl.ds(0, 16), 1), (1, pl.ds(16, 16), -1),
            (0, pl.ds(0, 32), 2),
        )[which]
        region = xs.at[(*block_index(gather_spot(k, s, q, shift)), rows, pl.ds(*GATHER_LANES[k]))]
        index = 4 * (s + q) + (2 if which == 4 else which)
        copy = pltpu.make_async_remote_copy(
            src_ref=region, dst_ref=region, send_sem=ga_s.at[k, index], recv_sem=ga_r.at[k, index],
            device_id=at(on_axis(GATHER_ORDER[k][s], step), c), device_id_type=MESH,
        )
        copy.start()
        gathers[k, s, q, which] = copy

    def direct(k, s, q):
        gather_copy(k, s, q, 0)
        gather_copy(k, s, q, 1)

    def forward(k, s, q):
        gathers[k, s, q, 0].wait_recv()
        gather_copy(k, s, q, 2)
        gathers[k, s, q, 1].wait_recv()
        gather_copy(k, s, q, 3)

    def finish(k, s, q):
        gathers[k, s, q, 2].wait_recv()
        gathers[k, s, q, 3].wait_recv()

    mine = block_index(me)
    for k in range(3):
        lanes = pl.ds(*GATHER_LANES[k])
        total = res_rows[:, lanes] + proj[h, :, lanes].astype(F32)
        for i in range(1, 8):
            head = (h + i) % 8
            proj_copy(k, head).wait_recv()
            total = total + proj_got[head, :, lanes].astype(F32)
        xs[(*mine, slice(None), lanes)] = total.astype(BF16)
        gather_copy(k, 0, 0, 4)
        direct(k, 0, 0)
    for k in range(3):
        for which in (0, 1, 4):
            gathers[k, 0, 0, which].wait_recv()
        direct(k, 1, 0)
    for k in range(3):
        direct(k, 2, 0)
    for k in range(3):
        forward(k, 1, 0)
    for k in range(3):
        direct(k, 2, 1)
        direct(k, 2, 2)
    for k in range(3):
        finish(k, 1, 0)
        direct(k, 2, 3)

    def feed(k, blocks):
        start, width = GATHER_LANES[k]
        total = None
        sums = square[...]
        for bxh, by in blocks:
            block = bxh * 4 + by
            pieces = []
            for t in range(start // 128, (start + width) // 128):
                part = xs[:, :, bxh, by, :, t * 128:(t + 1) * 128].reshape(256, 128).astype(F32)
                sums = sums + part * part
                scale = gains[2 * block + t // 4, t % 4:t % 4 + 1, :]
                pieces.append((part * scale).astype(BF16))
            scaled = jnp.concatenate(pieces, axis=1)
            depth = pl.ds(pl.multiple_of(block * 1024 + start, 128), width)
            term = lax.dot_general(gate_up[:, depth], scaled, NT, preferred_element_type=F32)
            total = term if total is None else total + term
        square[...] = sums
        acc[...] += total

    def feed_y(k, by):
        feed(k, ((0, by), (1, by)))

    def feed_x(k, bxh):
        def pair(i, _):
            feed(k, ((bxh, 2 * i), (bxh, 2 * i + 1)))
            return 0

        lax.fori_loop(0, 2, pair, 0)

    def feed_all(k):
        def pair(i, _):
            feed(k, ((0, i), (1, i)))
            return 0

        lax.fori_loop(0, 4, pair, 0)

    for copy in gain_copies:
        copy.wait()
    for i in (2, 3):
        loads[i].wait()
        swaps[i].wait()
    feed_y(0, y)
    for q in range(4):
        for k in (2, 0, 1):
            forward(k, 2, q)
    feed_y(0, (y + 1) % 4)
    feed_y(0, (y + 3) % 4)
    feed_x(1, xh)
    for q in range(4):
        finish(2, 2, q)
    feed_all(2)
    for q in range(4):
        finish(0, 2, q)
    feed_y(0, (y + 2) % 4)
    for q in range(4):
        finish(1, 2, q)
    feed_x(1, 1 - xh)

    norm = lax.rsqrt(jnp.sum(square[...].T, axis=0, keepdims=True) / D + 1e-05)
    gate = acc[0:2 * HID, :] * norm
    up = acc[2 * HID:4 * HID, :] * norm
    hidden[...] = (gate * jax.nn.sigmoid(gate) * up).T.astype(BF16)

    lane_low = lax.broadcasted_iota(jnp.int32, (256, 128), 1) < 64
    loads[4].wait()
    swaps[4].wait()

    scatters = {}

    def halves(k):
        start, count = SCATTER_ROWS[k]
        return ((start, count // 2), (start + count // 2, count // 2))

    def scatter_place(k, s, q, shift):
        order = SCATTER_ORDER[k]
        place = dict(me)
        if s == 0:
            place[order[1]] = (me[order[1]] + GROUPS[q] + 4) % 4
        place[order[s]] = (me[order[s]] + shift + 4) % 4
        if s < 2:
            place[order[2]] = None
        return place

    def scatter_copy(k, s, q, which):
        target, part, step = ((2, 0, 1), (2, 1, -1), (1, 1, 1), (-1, 0, -1), (1, 0, 1), (-1, 1, -1))[which]
        start, count = halves(k)[part]
        place = scatter_place(k, s, q, target)
        spot = kept_block(place, SCATTER_ORDER[k][s + 1:])
        if which < 2:
            dst = transit[k][s].at[(which, *spot)]
        else:
            side = 0 if step == 1 else 1
            dst = landing[k][s].at[(side, *spot, pl.ds(start - SCATTER_ROWS[k][0], count))]
        index = 24 * s + 6 * q + which
        copy = pltpu.make_async_remote_copy(
            src_ref=ys.at[(*block_index(place), pl.ds(start, count))],
            dst_ref=dst, send_sem=sc_s.at[k, index], recv_sem=sc_r.at[k, index],
            device_id=at(on_axis(SCATTER_ORDER[k][s], step), c), device_id_type=MESH,
        )
        copy.start()
        scatters[k, s, q, which] = copy

    def each_block(k, s, q, shift, body):
        order = SCATTER_ORDER[k]

        def one(block, _):
            place = scatter_place(k, s, q, shift)
            place[order[2]] = block
            body(block_index(place), kept_index(place, order[s + 1:]))
            return 0

        lax.fori_loop(0, 4, one, 0)

    def scatter_pass(k, s, q):
        for which, shift in ((0, 1), (1, -1)):
            scatters[k, s, q, which].wait_recv()
            rows = pl.ds(*halves(k)[which])

            def add(spot, kept_spot, which=which, rows=rows):
                both = ys[(*spot, rows)].astype(F32) + transit[k][s][(which, *kept_spot)].astype(F32)
                ys[(*spot, rows)] = both.astype(BF16)

            each_block(k, s, q, shift, add)
            scatter_copy(k, s, q, 4 + which)

    def scatter_end(k, s, q):
        for which in range(2, 6):
            scatters[k, s, q, which].wait_recv()
        rows = pl.ds(*SCATTER_ROWS[k])

        def add(spot, kept_spot):
            sums = ys[(*spot, rows)].astype(F32)
            for side in range(2):
                sums = sums + landing[k][s][(side, *kept_spot)].astype(F32)
            ys[(*spot, rows)] = sums.astype(BF16)

        each_block(k, s, q, 0, add)

    def last_copy(k, d):
        start, count = SCATTER_ROWS[k]
        axis = SCATTER_ORDER[k][2]
        copy = pltpu.make_async_remote_copy(
            src_ref=ys.at[(*block_index(on_axis(axis, d)), pl.ds(start, count))],
            dst_ref=landing[k][2].at[d - 1], send_sem=sc_s.at[k, 29 + d], recv_sem=sc_r.at[k, 29 + d],
            device_id=at(on_axis(axis, d), c), device_id_type=MESH,
        )
        copy.start()
        scatters[k, 2, 0, d] = copy

    for q in range(4):
        by = (y + GROUPS[q] + 4) % 4

        def project(bxh, _, by=by):
            col = pl.ds(pl.multiple_of((bxh * 4 + by) * 1024, 1024), 1024)
            wide = jnp.dot(hidden[...], down_all[:, col], preferred_element_type=F32)
            for pair in range(4):
                low = wide[:, pair * 128:(pair + 1) * 128]
                high = wide[:, 512 + pair * 128:512 + (pair + 1) * 128]
                first = jnp.where(lane_low, low, pltpu.roll(high, 64, 1)).astype(BF16)
                second = jnp.where(lane_low, pltpu.roll(low, 64, 1), high).astype(BF16)
                ys[pair // 2, (pair % 2) * 2, bxh, by] = first
                ys[pair // 2, (pair % 2) * 2 + 1, bxh, by] = second
            return 0

        lax.fori_loop(0, 2, project, 0)
        for which in range(4):
            scatter_copy(0, 0, q, which)
            scatter_copy(1, 0, q, which)
        for part in range(4):
            for which in ((0, 1), (3,), (2,), ())[q]:
                scatter_copy(2, 0, part, which)
    odd = h % 2
    tiles = []
    for core in range(2):
        window = pl.ds(pl.multiple_of(core * 512 + (h // 2) * 128, 128), 128)
        tiles.append(xs[:, :, xh, y, :, window].reshape(256, 128).astype(F32))
    even_pack = jnp.where(lane_low, tiles[0], pltpu.roll(tiles[1], 64, 1))
    odd_pack = jnp.where(lane_low, pltpu.roll(tiles[0], 64, 1), tiles[1])
    packed = jnp.where(odd == 0, even_pack, odd_pack)
    res_z[:, c] = packed.astype(BF16).reshape(8, 32, 128)
    res_copy = pltpu.make_async_remote_copy(
        src_ref=res_z.at[:, c], dst_ref=res_z.at[:, c], send_sem=fin_s.at[0], recv_sem=fin_r.at[0],
        device_id=sibling, device_id_type=MESH,
    )
    res_copy.start()

    for k in range(3):
        scatter_pass(k, 0, 0)
    for k in range(3):
        scatter_pass(k, 0, 1)
    for k in range(3):
        scatter_end(k, 0, 0)
        scatter_copy(k, 1, 0, 0)
        scatter_copy(k, 1, 0, 1)
    for k in range(3):
        scatter_pass(k, 0, 2)
    for k in range(3):
        scatter_end(k, 0, 1)
        scatter_copy(k, 1, 0, 3)
    for k in range(3):
        scatter_pass(k, 0, 3)
    for k in range(3):
        scatter_end(k, 0, 2)
        scatter_copy(k, 1, 0, 2)
    for k in range(3):
        scatter_pass(k, 1, 0)
    for k in range(3):
        scatter_end(k, 0, 3)
    for k in range(3):
        scatter_end(k, 1, 0)
        for d in (2, 1, 3):
            last_copy(k, d)
    for k in range(3):
        for i in range(1, 8):
            proj_copy(k, (h + i) % 8).wait_send()
    for copy in gathers.values():
        copy.wait_send()

    def give(i, copy, z_ref, out):
        copy.wait_send()
        copy.wait_recv()
        ordered = jnp.dot(perm[...], z_ref[...].reshape(512, 128), preferred_element_type=F32)
        ordered = jnp.where(c == 0, ordered, pltpu.roll(ordered, 64, 1))
        out[...] = ordered.T[0:64, :].astype(BF16)

    give(0, res_copy, res_z, res_out)
    for k in range(3):
        start, count = SCATTER_ROWS[k]
        sums = ys[(*block_index(me), pl.ds(start, count))].astype(F32)
        for d in range(1, 4):
            scatters[k, 2, 0, d].wait_recv()
            sums = sums + landing[k][2][d - 1].astype(F32)
        lay_z[start // 32:(start + count) // 32, c] = sums.astype(BF16).reshape(count // 32, 32, 128)
    lay_copy = pltpu.make_async_remote_copy(
        src_ref=lay_z.at[:, c], dst_ref=lay_z.at[:, c], send_sem=fin_s.at[1], recv_sem=fin_r.at[1],
        device_id=sibling, device_id_type=MESH,
    )
    lay_copy.start()
    for copy in scatters.values():
        copy.wait_send()
    give(1, lay_copy, lay_z, lay_out)


def layer(query, new_key, new_value, lengths, gain, slots, *hbm_args):
    vmem = pl.BlockSpec(memory_space=pltpu.VMEM)
    smem = pl.BlockSpec(memory_space=pltpu.SMEM)
    hbm = pl.BlockSpec(memory_space=pl.ANY)
    dma = pltpu.SemaphoreType.DMA
    landing, transit = [], []
    for k in range(3):
        for s in range(3):
            kept, count = kept_shape(SCATTER_ORDER[k][s + 1:]), SCATTER_ROWS[k][1]
            landing.append(pltpu.VMEM((3 if s == 2 else 2, *kept, count, 128), BF16))
            if s < 2:
                transit.append(pltpu.VMEM((2, *kept, count // 2, 128), BF16))
    return pl.pallas_call(
        layer_kernel,
        out_shape=[jax.ShapeDtypeStruct((64, 512), BF16)] * 2,
        in_specs=[vmem, vmem, vmem, smem, vmem, vmem] + [hbm] * len(hbm_args),
        out_specs=[vmem, vmem],
        scratch_shapes=[
            pltpu.VMEM((RING, CTX, HD), BF16),
            pltpu.VMEM((RING, CTX, HD), BF16),
            pltpu.VMEM((SLOTS, PER_KV, HD), F32),
            pltpu.VMEM((SLOTS, PER_KV, HD), F32),
            pltpu.VMEM((SLOTS, HD), F32),
            pltpu.VMEM((SLOTS, HD), F32),
            pltpu.VMEM((8, 128), F32),
            pltpu.VMEM((16, 8, 128), F32),
            pltpu.VMEM((8, 32, 1024), BF16),
            pltpu.VMEM((512, 512), BF16),
            pltpu.VMEM((512, 512), BF16),
            pltpu.VMEM((1024, 512), BF16),
            pltpu.VMEM((1024, 512), BF16),
            pltpu.VMEM((4 * HID, D), BF16),
            pltpu.VMEM((2 * HID, D), BF16),
            pltpu.VMEM((8, 32, 1024), BF16),
            pltpu.VMEM((8, 32, 1024), BF16),
            pltpu.VMEM((2, 4, 2, 4, 32, 1024), BF16),
            pltpu.VMEM((2, 4, 2, 4, 256, 128), BF16),
            pltpu.VMEM((4 * HID, 256), F32),
            pltpu.VMEM((256, 128), F32),
            pltpu.VMEM((512, 512), BF16),
            pltpu.VMEM((512, 128), F32),
            pltpu.VMEM((256, 2 * HID), BF16),
            pltpu.VMEM((8, 2, 32, 128), BF16),
            pltpu.VMEM((8, 2, 32, 128), BF16),
            pltpu.VMEM((32, 1024), F32),
            *landing,
            *transit,
            dma((2, RING)),
            dma((5,)),
            dma((5,)), dma((5,)),
            dma((2, 7)), dma((2, 7)),
            dma((15,)), dma((15,)),
            dma((3, 8)), dma((3, 8)),
            dma((3, 24)), dma((3, 24)),
            dma((3, 33)), dma((3, 33)),
            dma((2,)), dma((2,)),
        ],
        compiler_params=pltpu.CompilerParams(
            collective_id=0, has_side_effects=True, vmem_limit_bytes=58 * 2**20
        ),
        cost_estimate=pl.CostEstimate(flops=6 * 10**9, bytes_accessed=42 * 10**6, transcendentals=0),
        name="layer",
    )(query, new_key, new_value, lengths, gain, slots, *hbm_args)


def per_device(
    query,
    new_key,
    new_value,
    key_cache,
    value_cache,
    lengths,
    slot_row,
    resid,
    out_weight,
    norm_gain,
    gate_weight,
    up_weight,
    down_weight,
):
    residual, output = layer(
        query, new_key, new_value, lengths, norm_gain[None, :], slot_row[None, :],
        key_cache, value_cache, resid, out_weight, gate_weight.T, up_weight.T, down_weight,
    )
    return (residual.T, output.T)


def solution(mesh):
    placed = (
        P("grp", "head"),
        P("grp", "head"),
        P("grp", "head"),
        P("grp", "head", None, None),
        P("grp", "head", None, None),
        P("grp"),
        P(),
        P(None, "grp"),
        P("head", "grp"),
        P("grp"),
        P(None, ("grp", "head")),
        P(None, ("grp", "head")),
        P(("grp", "head"), None),
    )
    return jax.shard_map(
        per_device,
        mesh=mesh,
        in_specs=placed,
        out_specs=(P(None, ("grp", "head")), P(None, ("grp", "head"))),
        check_vma=False,
    )
```

```python
import jax
import jax.numpy as jnp
from jax import lax
from jax.experimental import pallas as pl
from jax.experimental.pallas import tpu as pltpu
from jax.sharding import PartitionSpec as P

D = 8192
HD = 128
PER_KV = 8
CTX = 1024
SLOTS = 32
HID = 224
RING = 8
UNROLL = 4
MESH = pl.DeviceIdType.MESH
BF16 = jnp.bfloat16
F32 = jnp.float32
NT = (((1,), (1,)), ((), ()))

GATHER_LANES = ((0, 384), (384, 384), (768, 256))
GATHER_ORDER = ("xzy", "yzx", "xyz")
SCATTER_ROWS = ((0, 96), (96, 96), (192, 64))
SCATTER_ORDER = ("zyx", "xyz", "yzx")
BESIDE = (0, -1, 1, 2)
GROUPS = (2, -1, 1, 0)


def device_at(x, y, z, c):
    return ((x // 2) * 8 + y * 2 + c, (x % 2) * 4 + z)


def block_index(where):
    x, y, z = where["x"], where["y"], where["z"]
    if x is None:
        xl, xh = slice(None), slice(None)
    else:
        xl, xh = x % 2, x // 2
    return (xl, slice(None) if z is None else z, xh, slice(None) if y is None else y)


def kept_index(where, kept):
    index = ()
    if "x" in kept:
        index += (where["x"] % 2,)
    if "z" in kept:
        index += (where["z"],)
    if "x" in kept:
        index += (where["x"] // 2,)
    if "y" in kept:
        index += (where["y"],)
    return index


def kept_block(where, kept):
    index = ()
    if "x" in kept:
        index += (slice(None) if where["x"] is None else where["x"] % 2,)
    if "z" in kept:
        index += (slice(None) if where["z"] is None else where["z"],)
    if "x" in kept:
        index += (slice(None) if where["x"] is None else where["x"] // 2,)
    if "y" in kept:
        index += (slice(None) if where["y"] is None else where["y"],)
    return index


def kept_shape(kept):
    shape = ()
    if "x" in kept:
        shape += (2,)
    if "z" in kept:
        shape += (4,)
    if "x" in kept:
        shape += (2,)
    if "y" in kept:
        shape += (4,)
    return shape


def layer_kernel(
    query, new_key, new_value, lengths, gain, slots, keys, values, resid, out_w, gate_w, up_w, down_w,
    both_out,
    key_ring, value_ring, score_ring, heads, mixed, new_key_f, new_value_f,
    gain_own, gains, got_att, resid_own, resid_sib, ow_own, ow_sib,
    gate_up, down_all,
    proj, proj_got, xs, ys, acc, square,
    perm, slot_col, hidden, res_z, lay_z, res_rows,
    *rest,
):
    landing = [[rest[k * 3 + s] for s in range(3)] for k in range(3)]
    transit = [[rest[9 + k * 2 + s] for s in range(2)] for k in range(3)]
    (kv_sem, load_sem, swap_s, swap_r, att_s, att_r, gain_s, gain_r, proj_s, proj_r,
     ga_s, ga_r, sc_s, sc_r, fin_s, fin_r) = rest[15:]

    g = lax.axis_index("grp")
    h = lax.axis_index("head")
    xh, y, c = g // 8, (g // 2) % 4, g % 2
    xl, z = h // 4, h % 4
    me = {"x": xh * 2 + xl, "y": y, "z": z}

    def on_axis(axis, step):
        place = dict(me)
        place[axis] = (me[axis] + step + 4) % 4
        return place

    def at(place, core):
        return device_at(place["x"], place["y"], place["z"], core)

    sibling = at(me, 1 - c)
    barrier = pltpu.get_barrier_semaphore()
    partners = []
    for i in range(1, 16):
        partners.append(((g + i) % 16, h))
    for i in range(1, 8):
        partners.append((g, (h + i) % 8))
    partners.append(((g + 8) % 16, (h + 4) % 8))
    for partner in partners:
        pl.semaphore_signal(barrier, inc=1, device_id=partner, device_id_type=MESH)

    def cache_copies(row, ring):
        return (
            pltpu.make_async_copy(keys.at[row, 0], key_ring.at[ring], kv_sem.at[0, ring]),
            pltpu.make_async_copy(values.at[row, 0], value_ring.at[ring], kv_sem.at[1, ring]),
        )

    for row in range(RING):
        for copy in cache_copies(row, row):
            copy.start()
    new_key_f[...] = new_key[...].astype(F32)
    new_value_f[...] = new_value[...].astype(F32)
    for j in range(PER_KV):
        heads[:, j, :] = query[:, j * HD:(j + 1) * HD].astype(F32)
    gain_own[0:4, :] = gain[...].astype(F32)
    gain_own[4:8, :] = jnp.zeros((4, 128), F32)
    spot_lane = lax.broadcasted_iota(jnp.int32, (PER_KV, CTX), 1)

    def rows_of(step):
        return [step * UNROLL + u for u in range(UNROLL)]

    def refill(which, step):
        for row in rows_of(step):

            @pl.when(row + RING < SLOTS)
            def _():
                cache_copies(row + RING, row % RING)[which].start()

    def score(step):
        found = []
        for row in rows_of(step):
            head = heads[row]
            part = lax.dot_general(
                head.astype(BF16), key_ring[row % RING], NT, preferred_element_type=F32
            ) * HD ** (-0.5)
            found.append(jnp.where(spot_lane < lengths[row], part, -1e30))
        return found

    def mix(step):
        group = rows_of(step)
        scores = [score_ring[step % 2, u] for u in range(UNROLL)]
        own = [
            jnp.sum(heads[row] * new_key_f[pl.ds(row, 1), :], axis=1, keepdims=True) * HD ** (-0.5)
            for row in group
        ]
        tops = [
            jnp.maximum(jnp.max(part, axis=1, keepdims=True), alone) for part, alone in zip(scores, own)
        ]
        weights = [jnp.exp(part - top) for part, top in zip(scores, tops)]
        own = [jnp.exp(alone - top) for alone, top in zip(own, tops)]
        shares = [
            1.0 / (jnp.sum(part, axis=1, keepdims=True) + alone) for part, alone in zip(weights, own)
        ]
        return [
            jnp.dot((part * share).astype(BF16), value_ring[row % RING], preferred_element_type=F32)
            + (alone * share).astype(BF16).astype(F32) * new_value_f[pl.ds(row, 1), :]
            for row, part, alone, share in zip(group, weights, own, shares)
        ]

    def attend(step, _):
        for row in rows_of(step + 1):
            cache_copies(row, row % RING)[0].wait()
        for row in rows_of(step):
            cache_copies(row, row % RING)[1].wait()
        coming = score(step + 1)
        for row, result in zip(rows_of(step), mix(step)):
            mixed[row] = result
        for u in range(UNROLL):
            score_ring[(step + 1) % 2, u] = coming[u]
        refill(0, step + 1)
        refill(1, step)
        return 0

    for row in rows_of(0):
        cache_copies(row, row % RING)[0].wait()
    for u, first in enumerate(score(0)):
        score_ring[0, u] = first
    refill(0, 0)
    swap_list = (
        (out_w, ow_sib), (resid, resid_sib), (gate_w, gate_up.at[pl.ds(HID, HID)]),
        (up_w, gate_up.at[pl.ds(3 * HID, HID)]), (down_w, down_all.at[pl.ds(HID, HID)]),
    )
    swaps = []

    def swap(i):
        copy = pltpu.make_async_remote_copy(
            src_ref=swap_list[i][0], dst_ref=swap_list[i][1], send_sem=swap_s.at[i], recv_sem=swap_r.at[i],
            device_id=sibling, device_id_type=MESH,
        )
        copy.start()
        swaps.append(copy)

    att_copies = []
    half = SLOTS // 2
    for part in range(2):
        steps = half // UNROLL
        lax.fori_loop(part * steps, (part + 1) * steps - part, attend, 0)
        if part == 1:
            last = 2 * steps - 1
            for row in rows_of(last):
                cache_copies(row, row % RING)[1].wait()
            for row, result in zip(rows_of(last), mix(last)):
                mixed[row] = result
        if part == 0:
            pl.semaphore_wait(barrier, len(partners))
        rows = pl.ds(part * half, half)
        for j in range(PER_KV):
            got_att[xh * 4 + y, rows, j * HD:(j + 1) * HD] = mixed[rows, j, :].astype(BF16)
        for i in (6, 5, 4, 2, 7, 3, 1):
            xy = ((xh + i // 4) % 2) * 4 + (y + i) % 4
            copy = pltpu.make_async_remote_copy(
                src_ref=got_att.at[xh * 4 + y, rows],
                dst_ref=got_att.at[xh * 4 + y, rows],
                send_sem=att_s.at[part, i - 1],
                recv_sem=att_r.at[part, i - 1],
                device_id=((xy // 4) * 8 + (xy % 4) * 2 + c, h),
                device_id_type=MESH,
            )
            copy.start()
            att_copies.append((i, copy))
        if part == 0:
            swap(0)
            swap(1)
    for i in range(2, 5):
        swap(i)
    gain_copies = []
    for i in range(1, 16):
        copy = pltpu.make_async_remote_copy(
            src_ref=gain_own,
            dst_ref=gains.at[g],
            send_sem=gain_s.at[i - 1],
            recv_sem=gain_r.at[i - 1],
            device_id=((g + i) % 16, h),
            device_id_type=MESH,
        )
        copy.start()
        gain_copies.append(copy)
    gains[g] = gain_own[...]
    loads = []
    for i, (src, dst) in enumerate(
        ((out_w, ow_own), (resid, resid_own), (gate_w, gate_up.at[pl.ds(0, HID)]),
         (up_w, gate_up.at[pl.ds(2 * HID, HID)]), (down_w, down_all.at[pl.ds(0, HID)]))
    ):
        copy = pltpu.make_async_copy(src, dst, load_sem.at[i])
        copy.start()
        loads.append(copy)

    slot_line = slots[...]
    for t in range(4):
        tile = jnp.broadcast_to(slot_line[:, t * 128:(t + 1) * 128].astype(F32), (128, 128))
        slot_col[t * 128:(t + 1) * 128, :] = tile.T
        batch = lax.broadcasted_iota(jnp.int32, (128, 512), 0) + t * 128
        perm[t * 128:(t + 1) * 128, :] = jnp.where(batch == slot_line, 1.0, 0.0).astype(BF16)
    square[...] = jnp.zeros_like(square)
    acc[...] = jnp.zeros_like(acc)

    loads[1].wait()
    swaps[1].wait()
    my_slots = slot_col[pl.ds(pl.multiple_of((2 * h + c) * 32, 32), 32), :]
    lane = lax.broadcasted_iota(jnp.int32, (32, 128), 1).astype(F32)
    pick = jnp.concatenate(
        [jnp.where(my_slots == lane + 128.0 * t, 1.0, 0.0).astype(BF16) for t in range(4)], axis=1
    )

    @pl.when(c == 0)
    def _():
        res_rows[:, 0:512] = jnp.dot(pick, resid_own[...], preferred_element_type=F32)
        res_rows[:, 512:1024] = jnp.dot(pick, resid_sib[...], preferred_element_type=F32)

    @pl.when(c == 1)
    def _():
        res_rows[:, 0:512] = jnp.dot(pick, resid_sib[...], preferred_element_type=F32)
        res_rows[:, 512:1024] = jnp.dot(pick, resid_own[...], preferred_element_type=F32)

    loads[0].wait()
    swaps[0].wait()
    for side in range(2):
        for i, copy in att_copies:
            if (i < 4) == (side == 0):
                copy.wait()
        xx = (xh + side) % 2
        part = got_att[pl.ds(xx * 4, 4)].reshape(128, 1024)
        own_part = jnp.dot(part, ow_own[...], preferred_element_type=F32).astype(BF16)
        sib_part = jnp.dot(part, ow_sib[...], preferred_element_type=F32).astype(BF16)
        proj[pl.ds(xx * 4, 4), :, pl.ds(pl.multiple_of(c * 512, 512), 512)] = own_part.reshape(4, 32, 512)
        proj[pl.ds(xx * 4, 4), :, pl.ds(pl.multiple_of((1 - c) * 512, 512), 512)] = sib_part.reshape(
            4, 32, 512
        )
        for k in range(3):
            lanes = pl.ds(*GATHER_LANES[k])
            for j in range(4):
                head = xx * 4 + (z + 2 + j) % 4

                @pl.when(head != h)
                def _():
                    pltpu.make_async_remote_copy(
                        src_ref=proj.at[head, :, lanes],
                        dst_ref=proj_got.at[h, :, lanes],
                        send_sem=proj_s.at[k, head],
                        recv_sem=proj_r.at[k, h],
                        device_id=(g, head),
                        device_id_type=MESH,
                    ).start()

    def proj_copy(k, head):
        lanes = pl.ds(*GATHER_LANES[k])
        return pltpu.make_async_remote_copy(
            src_ref=proj.at[head, :, lanes],
            dst_ref=proj_got.at[head, :, lanes],
            send_sem=proj_s.at[k, head],
            recv_sem=proj_r.at[k, head],
            device_id=(g, head),
            device_id_type=MESH,
        )

    gathers = {}

    def gather_spot(k, s, q, shift):
        order = GATHER_ORDER[k]
        place = dict(me)
        for a in order[:s]:
            place[a] = None
        if s == 2:
            place[order[1]] = (me[order[1]] + BESIDE[q] + 4) % 4
        place[order[s]] = (me[order[s]] + shift + 4) % 4
        return place

    def gather_copy(k, s, q, which):
        shift, rows, step = (
            (0, pl.ds(0, 32), 1), (0, pl.ds(0, 32), -1), (-1, pl.ds(0, 16), 1), (1, pl.ds(16, 16), -1),
            (0, pl.ds(0, 32), 2),
        )[which]
        region = xs.at[(*block_index(gather_spot(k, s, q, shift)), rows, pl.ds(*GATHER_LANES[k]))]
        index = 4 * (s + q) + (2 if which == 4 else which)
        copy = pltpu.make_async_remote_copy(
            src_ref=region, dst_ref=region, send_sem=ga_s.at[k, index], recv_sem=ga_r.at[k, index],
            device_id=at(on_axis(GATHER_ORDER[k][s], step), c), device_id_type=MESH,
        )
        copy.start()
        gathers[k, s, q, which] = copy

    def direct(k, s, q):
        gather_copy(k, s, q, 0)
        gather_copy(k, s, q, 1)

    def forward(k, s, q):
        gathers[k, s, q, 0].wait_recv()
        gather_copy(k, s, q, 2)
        gathers[k, s, q, 1].wait_recv()
        gather_copy(k, s, q, 3)

    def finish(k, s, q):
        gathers[k, s, q, 2].wait_recv()
        gathers[k, s, q, 3].wait_recv()

    mine = block_index(me)
    for k in range(3):
        lanes = pl.ds(*GATHER_LANES[k])
        total = res_rows[:, lanes] + proj[h, :, lanes].astype(F32)
        for i in range(1, 8):
            head = (h + i) % 8
            proj_copy(k, head).wait_recv()
            total = total + proj_got[head, :, lanes].astype(F32)
        xs[(*mine, slice(None), lanes)] = total.astype(BF16)
        gather_copy(k, 0, 0, 4)
        direct(k, 0, 0)
    for k in range(3):
        for which in (0, 1, 4):
            gathers[k, 0, 0, which].wait_recv()
        direct(k, 1, 0)
    for k in range(3):
        direct(k, 2, 0)
    for k in range(3):
        forward(k, 1, 0)
    for k in range(3):
        direct(k, 2, 1)
        direct(k, 2, 2)
    for k in range(3):
        finish(k, 1, 0)
        direct(k, 2, 3)

    def feed(k, blocks):
        start, width = GATHER_LANES[k]
        total = None
        sums = square[...]
        for bxh, by in blocks:
            block = bxh * 4 + by
            pieces = []
            for t in range(start // 128, (start + width) // 128):
                part = xs[:, :, bxh, by, :, t * 128:(t + 1) * 128].reshape(256, 128).astype(F32)
                sums = sums + part * part
                scale = gains[2 * block + t // 4, t % 4:t % 4 + 1, :]
                pieces.append((part * scale).astype(BF16))
            scaled = jnp.concatenate(pieces, axis=1)
            depth = pl.ds(pl.multiple_of(block * 1024 + start, 128), width)
            term = lax.dot_general(gate_up[:, depth], scaled, NT, preferred_element_type=F32)
            total = term if total is None else total + term
        square[...] = sums
        acc[...] += total

    def feed_y(k, by):
        feed(k, ((0, by), (1, by)))

    def feed_x(k, bxh):
        def pair(i, _):
            feed(k, ((bxh, 2 * i), (bxh, 2 * i + 1)))
            return 0

        lax.fori_loop(0, 2, pair, 0)

    def feed_all(k):
        def pair(i, _):
            feed(k, ((0, i), (1, i)))
            return 0

        lax.fori_loop(0, 4, pair, 0)

    for copy in gain_copies:
        copy.wait()
    for i in (2, 3):
        loads[i].wait()
        swaps[i].wait()
    feed_y(0, y)
    for q in range(4):
        for k in (2, 0, 1):
            forward(k, 2, q)
    feed_y(0, (y + 1) % 4)
    feed_y(0, (y + 3) % 4)
    feed_x(1, xh)
    for q in range(4):
        finish(2, 2, q)
    feed_all(2)
    for q in range(4):
        finish(0, 2, q)
    feed_y(0, (y + 2) % 4)
    for q in range(4):
        finish(1, 2, q)
    feed_x(1, 1 - xh)

    norm = lax.rsqrt(jnp.sum(square[...].T, axis=0, keepdims=True) / D + 1e-05)
    gate = acc[0:2 * HID, :] * norm
    up = acc[2 * HID:4 * HID, :] * norm
    hidden[...] = (gate * jax.nn.sigmoid(gate) * up).T.astype(BF16)

    lane_low = lax.broadcasted_iota(jnp.int32, (256, 128), 1) < 64
    loads[4].wait()
    swaps[4].wait()

    scatters = {}

    def halves(k):
        start, count = SCATTER_ROWS[k]
        return ((start, count // 2), (start + count // 2, count // 2))

    def scatter_place(k, s, q, shift):
        order = SCATTER_ORDER[k]
        place = dict(me)
        if s == 0:
            place[order[1]] = (me[order[1]] + GROUPS[q] + 4) % 4
        place[order[s]] = (me[order[s]] + shift + 4) % 4
        if s < 2:
            place[order[2]] = None
        return place

    def scatter_copy(k, s, q, which):
        target, part, step = ((2, 0, 1), (2, 1, -1), (1, 1, 1), (-1, 0, -1), (1, 0, 1), (-1, 1, -1))[which]
        start, count = halves(k)[part]
        place = scatter_place(k, s, q, target)
        spot = kept_block(place, SCATTER_ORDER[k][s + 1:])
        if which < 2:
            dst = transit[k][s].at[(which, *spot)]
        else:
            side = 0 if step == 1 else 1
            dst = landing[k][s].at[(side, *spot, pl.ds(start - SCATTER_ROWS[k][0], count))]
        index = 24 * s + 6 * q + which
        copy = pltpu.make_async_remote_copy(
            src_ref=ys.at[(*block_index(place), pl.ds(start, count))],
            dst_ref=dst, send_sem=sc_s.at[k, index], recv_sem=sc_r.at[k, index],
            device_id=at(on_axis(SCATTER_ORDER[k][s], step), c), device_id_type=MESH,
        )
        copy.start()
        scatters[k, s, q, which] = copy

    def each_block(k, s, q, shift):
        order = SCATTER_ORDER[k]
        found = []
        for block in range(4):
            place = scatter_place(k, s, q, shift)
            place[order[2]] = block
            found.append((block_index(place), kept_index(place, order[s + 1:])))
        return found

    def scatter_pass(k, s, q):
        for which, shift in ((0, 1), (1, -1)):
            scatters[k, s, q, which].wait_recv()
            rows = pl.ds(*halves(k)[which])
            found = each_block(k, s, q, shift)
            sums = [
                ys[(*spot, rows)].astype(F32) + transit[k][s][(which, *kept_spot)].astype(F32)
                for spot, kept_spot in found
            ]
            for (spot, _), both in zip(found, sums):
                ys[(*spot, rows)] = both.astype(BF16)
            scatter_copy(k, s, q, 4 + which)

    def scatter_end(k, s, q):
        for which in range(2, 6):
            scatters[k, s, q, which].wait_recv()
        rows = pl.ds(*SCATTER_ROWS[k])
        found = each_block(k, s, q, 0)
        sums = [
            (
                ys[(*spot, rows)].astype(F32)
                + landing[k][s][(0, *kept_spot)].astype(F32)
                + landing[k][s][(1, *kept_spot)].astype(F32)
            ).astype(BF16)
            for spot, kept_spot in found
        ]
        for (spot, _), both in zip(found, sums):
            ys[(*spot, rows)] = both

    def near(q):
        for which in (2, 3):
            scatter_copy(0, 0, q, which)
            scatter_copy(1, 0, q, which)

    def last_copy(k, d):
        start, count = SCATTER_ROWS[k]
        axis = SCATTER_ORDER[k][2]
        copy = pltpu.make_async_remote_copy(
            src_ref=ys.at[(*block_index(on_axis(axis, d)), pl.ds(start, count))],
            dst_ref=landing[k][2].at[d - 1], send_sem=sc_s.at[k, 29 + d], recv_sem=sc_r.at[k, 29 + d],
            device_id=at(on_axis(axis, d), c), device_id_type=MESH,
        )
        copy.start()
        scatters[k, 2, 0, d] = copy

    for q in range(4):
        by = (y + GROUPS[q] + 4) % 4

        def project(bxh, _, by=by):
            col = pl.ds(pl.multiple_of((bxh * 4 + by) * 1024, 1024), 1024)
            wide = jnp.dot(hidden[...], down_all[:, col], preferred_element_type=F32)
            for pair in range(4):
                low = wide[:, pair * 128:(pair + 1) * 128]
                high = wide[:, 512 + pair * 128:512 + (pair + 1) * 128]
                first = jnp.where(lane_low, low, pltpu.roll(high, 64, 1)).astype(BF16)
                second = jnp.where(lane_low, pltpu.roll(low, 64, 1), high).astype(BF16)
                ys[pair // 2, (pair % 2) * 2, bxh, by] = first
                ys[pair // 2, (pair % 2) * 2 + 1, bxh, by] = second
            return 0

        lax.fori_loop(0, 2, project, 0)
        for which in range(2):
            scatter_copy(0, 0, q, which)
            scatter_copy(1, 0, q, which)
        for part in range(4):
            for which in ((0, 1), (3,), (2,), ())[q]:
                scatter_copy(2, 0, part, which)
    odd = h % 2
    tiles = []
    for core in range(2):
        window = pl.ds(pl.multiple_of(core * 512 + (h // 2) * 128, 128), 128)
        tiles.append(xs[:, :, xh, y, :, window].reshape(256, 128).astype(F32))
    even_pack = jnp.where(lane_low, tiles[0], pltpu.roll(tiles[1], 64, 1))
    odd_pack = jnp.where(lane_low, pltpu.roll(tiles[0], 64, 1), tiles[1])
    packed = jnp.where(odd == 0, even_pack, odd_pack)
    res_z[:, c] = packed.astype(BF16).reshape(8, 32, 128)
    res_copy = pltpu.make_async_remote_copy(
        src_ref=res_z.at[:, c], dst_ref=res_z.at[:, c], send_sem=fin_s.at[0], recv_sem=fin_r.at[0],
        device_id=sibling, device_id_type=MESH,
    )
    res_copy.start()

    near(0)
    for k in range(3):
        scatter_pass(k, 0, 0)
    near(1)
    for k in range(3):
        scatter_pass(k, 0, 1)
    near(2)
    for k in range(3):
        scatter_end(k, 0, 0)
        scatter_copy(k, 1, 0, 0)
        scatter_copy(k, 1, 0, 1)
    for k in range(3):
        scatter_pass(k, 0, 2)
    near(3)
    for k in range(3):
        scatter_end(k, 0, 1)
        scatter_copy(k, 1, 0, 3)
    for k in range(3):
        scatter_pass(k, 0, 3)
    for k in range(3):
        scatter_end(k, 0, 2)
        scatter_copy(k, 1, 0, 2)
    for k in range(3):
        scatter_pass(k, 1, 0)
    for k in range(3):
        scatter_end(k, 0, 3)
    for k in range(3):
        scatter_end(k, 1, 0)
        for d in (2, 1, 3):
            last_copy(k, d)
    for k in range(3):
        for i in range(1, 8):
            proj_copy(k, (h + i) % 8).wait_send()
    for copy in gathers.values():
        copy.wait_send()

    def give(i, copy, z_ref):
        copy.wait_send()
        copy.wait_recv()
        ordered = jnp.dot(perm[...], z_ref[...].reshape(512, 128), preferred_element_type=F32)
        ordered = jnp.where(c == 0, ordered, pltpu.roll(ordered, 64, 1))
        both_out[i] = ordered.T[0:64, :].astype(BF16)

    give(0, res_copy, res_z)
    for k in range(3):
        start, count = SCATTER_ROWS[k]
        sums = ys[(*block_index(me), pl.ds(start, count))].astype(F32)
        for d in range(1, 4):
            scatters[k, 2, 0, d].wait_recv()
            sums = sums + landing[k][2][d - 1].astype(F32)
        lay_z[start // 32:(start + count) // 32, c] = sums.astype(BF16).reshape(count // 32, 32, 128)
    lay_copy = pltpu.make_async_remote_copy(
        src_ref=lay_z.at[:, c], dst_ref=lay_z.at[:, c], send_sem=fin_s.at[1], recv_sem=fin_r.at[1],
        device_id=sibling, device_id_type=MESH,
    )
    lay_copy.start()
    for copy in scatters.values():
        copy.wait_send()
    give(1, lay_copy, lay_z)


def layer(query, new_key, new_value, lengths, gain, slots, *hbm_args):
    vmem = pl.BlockSpec(memory_space=pltpu.VMEM)
    smem = pl.BlockSpec(memory_space=pltpu.SMEM)
    hbm = pl.BlockSpec(memory_space=pl.ANY)
    dma = pltpu.SemaphoreType.DMA
    landing, transit = [], []
    for k in range(3):
        for s in range(3):
            kept, count = kept_shape(SCATTER_ORDER[k][s + 1:]), SCATTER_ROWS[k][1]
            landing.append(pltpu.VMEM((3 if s == 2 else 2, *kept, count, 128), BF16))
            if s < 2:
                transit.append(pltpu.VMEM((2, *kept, count // 2, 128), BF16))
    return pl.pallas_call(
        layer_kernel,
        out_shape=jax.ShapeDtypeStruct((2, 64, 512), BF16),
        in_specs=[vmem, vmem, vmem, smem, vmem, vmem] + [hbm] * len(hbm_args),
        out_specs=vmem,
        scratch_shapes=[
            pltpu.VMEM((RING, CTX, HD), BF16),
            pltpu.VMEM((RING, CTX, HD), BF16),
            pltpu.VMEM((2, UNROLL, PER_KV, CTX), F32),
            pltpu.VMEM((SLOTS, PER_KV, HD), F32),
            pltpu.VMEM((SLOTS, PER_KV, HD), F32),
            pltpu.VMEM((SLOTS, HD), F32),
            pltpu.VMEM((SLOTS, HD), F32),
            pltpu.VMEM((8, 128), F32),
            pltpu.VMEM((16, 8, 128), F32),
            pltpu.VMEM((8, 32, 1024), BF16),
            pltpu.VMEM((512, 512), BF16),
            pltpu.VMEM((512, 512), BF16),
            pltpu.VMEM((1024, 512), BF16),
            pltpu.VMEM((1024, 512), BF16),
            pltpu.VMEM((4 * HID, D), BF16),
            pltpu.VMEM((2 * HID, D), BF16),
            pltpu.VMEM((8, 32, 1024), BF16),
            pltpu.VMEM((8, 32, 1024), BF16),
            pltpu.VMEM((2, 4, 2, 4, 32, 1024), BF16),
            pltpu.VMEM((2, 4, 2, 4, 256, 128), BF16),
            pltpu.VMEM((4 * HID, 256), F32),
            pltpu.VMEM((256, 128), F32),
            pltpu.VMEM((512, 512), BF16),
            pltpu.VMEM((512, 128), F32),
            pltpu.VMEM((256, 2 * HID), BF16),
            pltpu.VMEM((8, 2, 32, 128), BF16),
            pltpu.VMEM((8, 2, 32, 128), BF16),
            pltpu.VMEM((32, 1024), F32),
            *landing,
            *transit,
            dma((2, RING)),
            dma((5,)),
            dma((5,)), dma((5,)),
            dma((2, 7)), dma((2, 7)),
            dma((15,)), dma((15,)),
            dma((3, 8)), dma((3, 8)),
            dma((3, 24)), dma((3, 24)),
            dma((3, 33)), dma((3, 33)),
            dma((2,)), dma((2,)),
        ],
        compiler_params=pltpu.CompilerParams(
            collective_id=0, has_side_effects=True, vmem_limit_bytes=58 * 2**20
        ),
        cost_estimate=pl.CostEstimate(flops=6 * 10**9, bytes_accessed=42 * 10**6, transcendentals=0),
        name="layer",
    )(query, new_key, new_value, lengths, gain, slots, *hbm_args)


def per_device(
    query,
    new_key,
    new_value,
    key_cache,
    value_cache,
    lengths,
    slot_row,
    resid,
    out_weight,
    norm_gain,
    gate_weight,
    up_weight,
    down_weight,
):
    both = layer(
        query, new_key, new_value, lengths, norm_gain.reshape(4, 128), slot_row[None, :],
        key_cache, value_cache, resid, out_weight, gate_weight.T, up_weight.T, down_weight,
    )
    return (both[0].T, both[1].T)


def solution(mesh):
    placed = (
        P("grp", "head"),
        P("grp", "head"),
        P("grp", "head"),
        P("grp", "head", None, None),
        P("grp", "head", None, None),
        P("grp"),
        P(),
        P(None, "grp"),
        P("head", "grp"),
        P("grp"),
        P(None, ("grp", "head")),
        P(None, ("grp", "head")),
        P(("grp", "head"), None),
    )
    return jax.shard_map(
        per_device,
        mesh=mesh,
        in_specs=placed,
        out_specs=(P(None, ("grp", "head")), P(None, ("grp", "head"))),
        check_vma=False,
    )
```

```python
import jax
import jax.numpy as jnp
from jax import lax
from jax.experimental import pallas as pl
from jax.experimental.pallas import tpu as pltpu
from jax.sharding import PartitionSpec as P

D = 8192
HD = 128
PER_KV = 8
CTX = 1024
SLOTS = 32
HID = 224
RING = 8
UNROLL = 4
MESH = pl.DeviceIdType.MESH
BF16 = jnp.bfloat16
F32 = jnp.float32
NT = (((1,), (1,)), ((), ()))

GATHER_LANES = ((0, 384), (384, 384), (768, 256))
GATHER_ORDER = ("xzy", "yzx", "xyz")
SCATTER_ROWS = ((0, 96), (96, 96), (192, 64))
SCATTER_ORDER = ("zyx", "xyz", "yzx")
BESIDE = (0, -1, 1, 2)
GROUPS = (2, -1, 1, 0)


def device_at(x, y, z, c):
    return ((x // 2) * 8 + y * 2 + c, (x % 2) * 4 + z)


def block_index(where):
    x, y, z = where["x"], where["y"], where["z"]
    if x is None:
        xl, xh = slice(None), slice(None)
    else:
        xl, xh = x % 2, x // 2
    return (xl, slice(None) if z is None else z, xh, slice(None) if y is None else y)


def kept_index(where, kept):
    index = ()
    if "x" in kept:
        index += (where["x"] % 2,)
    if "z" in kept:
        index += (where["z"],)
    if "x" in kept:
        index += (where["x"] // 2,)
    if "y" in kept:
        index += (where["y"],)
    return index


def kept_block(where, kept):
    index = ()
    if "x" in kept:
        index += (slice(None) if where["x"] is None else where["x"] % 2,)
    if "z" in kept:
        index += (slice(None) if where["z"] is None else where["z"],)
    if "x" in kept:
        index += (slice(None) if where["x"] is None else where["x"] // 2,)
    if "y" in kept:
        index += (slice(None) if where["y"] is None else where["y"],)
    return index


def kept_shape(kept):
    shape = ()
    if "x" in kept:
        shape += (2,)
    if "z" in kept:
        shape += (4,)
    if "x" in kept:
        shape += (2,)
    if "y" in kept:
        shape += (4,)
    return shape


def layer_kernel(
    query, new_key, new_value, lengths, gain, slots, keys, values, resid, out_w, gate_w, up_w, down_w,
    both_out,
    key_ring, value_ring, score_ring, heads, mixed, new_key_f, new_value_f,
    gain_own, gains, got_att, resid_own, resid_sib, ow_own, ow_sib,
    gate_up, down_all,
    proj, proj_got, xs, ys, acc, square,
    perm, slot_col, hidden, res_z, lay_z, res_rows,
    *rest,
):
    landing = [[rest[k * 3 + s] for s in range(3)] for k in range(3)]
    transit = [[rest[9 + k * 2 + s] for s in range(2)] for k in range(3)]
    (kv_sem, load_sem, swap_s, swap_r, att_s, att_r, gain_s, gain_r, proj_s, proj_r,
     ga_s, ga_r, sc_s, sc_r, fin_s, fin_r) = rest[15:]

    g = lax.axis_index("grp")
    h = lax.axis_index("head")
    xh, y, c = g // 8, (g // 2) % 4, g % 2
    xl, z = h // 4, h % 4
    me = {"x": xh * 2 + xl, "y": y, "z": z}

    def on_axis(axis, step):
        place = dict(me)
        place[axis] = (me[axis] + step + 4) % 4
        return place

    def at(place, core):
        return device_at(place["x"], place["y"], place["z"], core)

    sibling = at(me, 1 - c)
    barrier = pltpu.get_barrier_semaphore()
    partners = []
    for i in range(1, 16):
        partners.append(((g + i) % 16, h))
    for i in range(1, 8):
        partners.append((g, (h + i) % 8))
    partners.append(((g + 8) % 16, (h + 4) % 8))
    for partner in partners:
        pl.semaphore_signal(barrier, inc=1, device_id=partner, device_id_type=MESH)

    def cache_copies(row, ring):
        return (
            pltpu.make_async_copy(keys.at[row, 0], key_ring.at[ring], kv_sem.at[0, ring]),
            pltpu.make_async_copy(values.at[row, 0], value_ring.at[ring], kv_sem.at[1, ring]),
        )

    for row in range(RING):
        for copy in cache_copies(row, row):
            copy.start()
    new_key_f[...] = new_key[...].astype(F32)
    new_value_f[...] = new_value[...].astype(F32)
    for j in range(PER_KV):
        heads[:, j, :] = query[:, j * HD:(j + 1) * HD].astype(F32)
    gain_own[0:4, :] = gain[...].astype(F32)
    gain_own[4:8, :] = jnp.zeros((4, 128), F32)
    spot_lane = lax.broadcasted_iota(jnp.int32, (PER_KV, CTX), 1)

    def rows_of(step):
        return [step * UNROLL + u for u in range(UNROLL)]

    def refill(which, step):
        for row in rows_of(step):

            @pl.when(row + RING < SLOTS)
            def _():
                cache_copies(row + RING, row % RING)[which].start()

    def score(step):
        found = []
        for row in rows_of(step):
            head = heads[row]
            part = lax.dot_general(
                head.astype(BF16), key_ring[row % RING], NT, preferred_element_type=F32
            ) * HD ** (-0.5)
            found.append(jnp.where(spot_lane < lengths[row], part, -1e30))
        return found

    def mix(step):
        group = rows_of(step)
        scores = [score_ring[step % 2, u] for u in range(UNROLL)]
        own = [
            jnp.sum(heads[row] * new_key_f[pl.ds(row, 1), :], axis=1, keepdims=True) * HD ** (-0.5)
            for row in group
        ]
        tops = [
            jnp.maximum(jnp.max(part, axis=1, keepdims=True), alone) for part, alone in zip(scores, own)
        ]
        weights = [jnp.exp(part - top) for part, top in zip(scores, tops)]
        own = [jnp.exp(alone - top) for alone, top in zip(own, tops)]
        shares = [
            1.0 / (jnp.sum(part, axis=1, keepdims=True) + alone) for part, alone in zip(weights, own)
        ]
        return [
            jnp.dot((part * share).astype(BF16), value_ring[row % RING], preferred_element_type=F32)
            + (alone * share).astype(BF16).astype(F32) * new_value_f[pl.ds(row, 1), :]
            for row, part, alone, share in zip(group, weights, own, shares)
        ]

    def attend(step, _):
        for row in rows_of(step + 1):
            cache_copies(row, row % RING)[0].wait()
        for row in rows_of(step):
            cache_copies(row, row % RING)[1].wait()
        coming = score(step + 1)
        for row, result in zip(rows_of(step), mix(step)):
            mixed[row] = result
        for u in range(UNROLL):
            score_ring[(step + 1) % 2, u] = coming[u]
        refill(0, step + 1)
        refill(1, step)
        return 0

    for row in rows_of(0):
        cache_copies(row, row % RING)[0].wait()
    for u, first in enumerate(score(0)):
        score_ring[0, u] = first
    refill(0, 0)
    swap_list = (
        (out_w, ow_sib), (resid, resid_sib), (gate_w, gate_up.at[pl.ds(HID, HID)]),
        (up_w, gate_up.at[pl.ds(3 * HID, HID)]), (down_w, down_all.at[pl.ds(HID, HID)]),
    )
    swaps = []

    def swap(i):
        copy = pltpu.make_async_remote_copy(
            src_ref=swap_list[i][0], dst_ref=swap_list[i][1], send_sem=swap_s.at[i], recv_sem=swap_r.at[i],
            device_id=sibling, device_id_type=MESH,
        )
        copy.start()
        swaps.append(copy)

    att_copies = []
    half = SLOTS // 2
    for part in range(2):
        steps = half // UNROLL
        lax.fori_loop(part * steps, (part + 1) * steps - part, attend, 0)
        if part == 1:
            last = 2 * steps - 1
            for row in rows_of(last):
                cache_copies(row, row % RING)[1].wait()
            for row, result in zip(rows_of(last), mix(last)):
                mixed[row] = result
        if part == 0:
            pl.semaphore_wait(barrier, len(partners))
        rows = pl.ds(part * half, half)
        for j in range(PER_KV):
            got_att[xh * 4 + y, rows, j * HD:(j + 1) * HD] = mixed[rows, j, :].astype(BF16)
        for i in (6, 5, 4, 2, 7, 3, 1):
            xy = ((xh + i // 4) % 2) * 4 + (y + i) % 4
            copy = pltpu.make_async_remote_copy(
                src_ref=got_att.at[xh * 4 + y, rows],
                dst_ref=got_att.at[xh * 4 + y, rows],
                send_sem=att_s.at[part, i - 1],
                recv_sem=att_r.at[part, i - 1],
                device_id=((xy // 4) * 8 + (xy % 4) * 2 + c, h),
                device_id_type=MESH,
            )
            copy.start()
            att_copies.append((i, copy))
        if part == 0:
            swap(0)
            swap(1)
    for i in range(2, 5):
        swap(i)
    gain_copies = []
    for i in range(1, 16):
        copy = pltpu.make_async_remote_copy(
            src_ref=gain_own,
            dst_ref=gains.at[g],
            send_sem=gain_s.at[i - 1],
            recv_sem=gain_r.at[i - 1],
            device_id=((g + i) % 16, h),
            device_id_type=MESH,
        )
        copy.start()
        gain_copies.append(copy)
    gains[g] = gain_own[...]
    loads = []
    for i, (src, dst) in enumerate(
        ((out_w, ow_own), (resid, resid_own), (gate_w, gate_up.at[pl.ds(0, HID)]),
         (up_w, gate_up.at[pl.ds(2 * HID, HID)]), (down_w, down_all.at[pl.ds(0, HID)]))
    ):
        copy = pltpu.make_async_copy(src, dst, load_sem.at[i])
        copy.start()
        loads.append(copy)

    slot_line = slots[...]
    for t in range(4):
        tile = jnp.broadcast_to(slot_line[:, t * 128:(t + 1) * 128].astype(F32), (128, 128))
        slot_col[t * 128:(t + 1) * 128, :] = tile.T
        batch = lax.broadcasted_iota(jnp.int32, (128, 512), 0) + t * 128
        perm[t * 128:(t + 1) * 128, :] = jnp.where(batch == slot_line, 1.0, 0.0).astype(BF16)
    square[...] = jnp.zeros_like(square)
    acc[...] = jnp.zeros_like(acc)

    loads[1].wait()
    swaps[1].wait()
    my_slots = slot_col[pl.ds(pl.multiple_of((2 * h + c) * 32, 32), 32), :]
    lane = lax.broadcasted_iota(jnp.int32, (32, 128), 1).astype(F32)
    pick = jnp.concatenate(
        [jnp.where(my_slots == lane + 128.0 * t, 1.0, 0.0).astype(BF16) for t in range(4)], axis=1
    )

    @pl.when(c == 0)
    def _():
        res_rows[:, 0:512] = jnp.dot(pick, resid_own[...], preferred_element_type=F32)
        res_rows[:, 512:1024] = jnp.dot(pick, resid_sib[...], preferred_element_type=F32)

    @pl.when(c == 1)
    def _():
        res_rows[:, 0:512] = jnp.dot(pick, resid_sib[...], preferred_element_type=F32)
        res_rows[:, 512:1024] = jnp.dot(pick, resid_own[...], preferred_element_type=F32)

    loads[0].wait()
    swaps[0].wait()
    for side in range(2):
        for i, copy in att_copies:
            if (i < 4) == (side == 0):
                copy.wait()
        xx = (xh + side) % 2
        part = got_att[pl.ds(xx * 4, 4)].reshape(128, 1024)
        own_part = jnp.dot(part, ow_own[...], preferred_element_type=F32).astype(BF16)
        sib_part = jnp.dot(part, ow_sib[...], preferred_element_type=F32).astype(BF16)
        proj[pl.ds(xx * 4, 4), :, pl.ds(pl.multiple_of(c * 512, 512), 512)] = own_part.reshape(4, 32, 512)
        proj[pl.ds(xx * 4, 4), :, pl.ds(pl.multiple_of((1 - c) * 512, 512), 512)] = sib_part.reshape(
            4, 32, 512
        )
        for k in range(3):
            lanes = pl.ds(*GATHER_LANES[k])
            for j in range(4):
                head = xx * 4 + (z + 2 + j) % 4

                @pl.when(head != h)
                def _():
                    pltpu.make_async_remote_copy(
                        src_ref=proj.at[head, :, lanes],
                        dst_ref=proj_got.at[h, :, lanes],
                        send_sem=proj_s.at[k, head],
                        recv_sem=proj_r.at[k, h],
                        device_id=(g, head),
                        device_id_type=MESH,
                    ).start()

    def proj_copy(k, head):
        lanes = pl.ds(*GATHER_LANES[k])
        return pltpu.make_async_remote_copy(
            src_ref=proj.at[head, :, lanes],
            dst_ref=proj_got.at[head, :, lanes],
            send_sem=proj_s.at[k, head],
            recv_sem=proj_r.at[k, head],
            device_id=(g, head),
            device_id_type=MESH,
        )

    gathers = {}

    def gather_spot(k, s, q, shift):
        order = GATHER_ORDER[k]
        place = dict(me)
        for a in order[:s]:
            place[a] = None
        if s == 2:
            place[order[1]] = (me[order[1]] + BESIDE[q] + 4) % 4
        place[order[s]] = (me[order[s]] + shift + 4) % 4
        return place

    def gather_copy(k, s, q, which):
        shift, rows, step = (
            (0, pl.ds(0, 32), 1), (0, pl.ds(0, 32), -1), (-1, pl.ds(0, 16), 1), (1, pl.ds(16, 16), -1),
            (0, pl.ds(0, 32), 2),
        )[which]
        region = xs.at[(*block_index(gather_spot(k, s, q, shift)), rows, pl.ds(*GATHER_LANES[k]))]
        index = 4 * (s + q) + (2 if which == 4 else which)
        copy = pltpu.make_async_remote_copy(
            src_ref=region, dst_ref=region, send_sem=ga_s.at[k, index], recv_sem=ga_r.at[k, index],
            device_id=at(on_axis(GATHER_ORDER[k][s], step), c), device_id_type=MESH,
        )
        copy.start()
        gathers[k, s, q, which] = copy

    def direct(k, s, q):
        gather_copy(k, s, q, 0)
        gather_copy(k, s, q, 1)

    def forward(k, s, q):
        gathers[k, s, q, 0].wait_recv()
        gather_copy(k, s, q, 2)
        gathers[k, s, q, 1].wait_recv()
        gather_copy(k, s, q, 3)

    def finish(k, s, q):
        gathers[k, s, q, 2].wait_recv()
        gathers[k, s, q, 3].wait_recv()

    mine = block_index(me)
    for k in range(3):
        lanes = pl.ds(*GATHER_LANES[k])
        total = res_rows[:, lanes] + proj[h, :, lanes].astype(F32)
        for i in range(1, 8):
            head = (h + i) % 8
            proj_copy(k, head).wait_recv()
            total = total + proj_got[head, :, lanes].astype(F32)
        xs[(*mine, slice(None), lanes)] = total.astype(BF16)
        gather_copy(k, 0, 0, 4)
        direct(k, 0, 0)
    for k in range(3):
        for which in (0, 1, 4):
            gathers[k, 0, 0, which].wait_recv()
        gather_copy(k, 1, 0, 4)
        direct(k, 1, 0)
    for k in range(3):
        direct(k, 2, 0)
    for k in range(3):
        gathers[k, 1, 0, 0].wait_recv()
        direct(k, 2, 1)
        gathers[k, 1, 0, 1].wait_recv()
        direct(k, 2, 2)
    for k in range(3):
        gathers[k, 1, 0, 4].wait_recv()
        direct(k, 2, 3)

    def feed(k, blocks):
        start, width = GATHER_LANES[k]
        total = None
        sums = square[...]
        for bxh, by in blocks:
            block = bxh * 4 + by
            pieces = []
            for t in range(start // 128, (start + width) // 128):
                part = xs[:, :, bxh, by, :, t * 128:(t + 1) * 128].reshape(256, 128)
                scale = gains[2 * block + t // 4, t % 4:t % 4 + 1, :].astype(BF16)
                pieces.append(part * scale)
                part = part.astype(F32)
                sums = sums + part * part
            scaled = jnp.concatenate(pieces, axis=1)
            depth = pl.ds(pl.multiple_of(block * 1024 + start, 128), width)
            term = lax.dot_general(gate_up[:, depth], scaled, NT, preferred_element_type=F32)
            total = term if total is None else total + term
        square[...] = sums
        acc[...] += total

    def feed_y(k, by):
        feed(k, ((0, by), (1, by)))

    def feed_x(k, bxh):
        def pair(i, _):
            feed(k, ((bxh, 2 * i), (bxh, 2 * i + 1)))
            return 0

        lax.fori_loop(0, 2, pair, 0)

    def feed_all(k):
        def pair(i, _):
            feed(k, ((0, i), (1, i)))
            return 0

        lax.fori_loop(0, 4, pair, 0)

    for copy in gain_copies:
        copy.wait()
    for i in (2, 3):
        loads[i].wait()
        swaps[i].wait()
    feed_y(0, y)
    for q in range(4):
        for k in (2, 0, 1):
            forward(k, 2, q)
    feed_y(0, (y + 1) % 4)
    feed_y(0, (y + 3) % 4)
    feed_x(1, xh)
    for q in range(4):
        finish(2, 2, q)
    feed_all(2)
    for q in range(4):
        finish(0, 2, q)
    feed_y(0, (y + 2) % 4)
    for q in range(4):
        finish(1, 2, q)
    feed_x(1, 1 - xh)

    norm = lax.rsqrt(jnp.sum(square[...].T, axis=0, keepdims=True) / D + 1e-05)
    gate = acc[0:2 * HID, :] * norm
    up = acc[2 * HID:4 * HID, :] * norm
    hidden[...] = (gate * jax.nn.sigmoid(gate) * up).T.astype(BF16)

    lane_low = lax.broadcasted_iota(jnp.int32, (256, 128), 1) < 64
    loads[4].wait()
    swaps[4].wait()

    scatters = {}

    def halves(k):
        start, count = SCATTER_ROWS[k]
        return ((start, count // 2), (start + count // 2, count // 2))

    def scatter_place(k, s, q, shift):
        order = SCATTER_ORDER[k]
        place = dict(me)
        if s == 0:
            place[order[1]] = (me[order[1]] + GROUPS[q] + 4) % 4
        place[order[s]] = (me[order[s]] + shift + 4) % 4
        if s < 2:
            place[order[2]] = None
        return place

    def scatter_copy(k, s, q, which):
        target, part, step = ((2, 0, 1), (2, 1, -1), (1, 1, 1), (-1, 0, -1), (1, 0, 1), (-1, 1, -1))[which]
        start, count = halves(k)[part]
        place = scatter_place(k, s, q, target)
        spot = kept_block(place, SCATTER_ORDER[k][s + 1:])
        if which < 2:
            dst = transit[k][s].at[(which, *spot)]
        else:
            side = 0 if step == 1 else 1
            dst = landing[k][s].at[(side, *spot, pl.ds(start - SCATTER_ROWS[k][0], count))]
        index = 24 * s + 6 * q + which
        copy = pltpu.make_async_remote_copy(
            src_ref=ys.at[(*block_index(place), pl.ds(start, count))],
            dst_ref=dst, send_sem=sc_s.at[k, index], recv_sem=sc_r.at[k, index],
            device_id=at(on_axis(SCATTER_ORDER[k][s], step), c), device_id_type=MESH,
        )
        copy.start()
        scatters[k, s, q, which] = copy

    def each_block(k, s, q, shift):
        order = SCATTER_ORDER[k]
        found = []
        for block in range(4):
            place = scatter_place(k, s, q, shift)
            place[order[2]] = block
            found.append((block_index(place), kept_index(place, order[s + 1:])))
        return found

    def scatter_pass(k, s, q):
        for which, shift in ((0, 1), (1, -1)):
            scatters[k, s, q, which].wait_recv()
            rows = pl.ds(*halves(k)[which])
            found = each_block(k, s, q, shift)
            sums = [
                ys[(*spot, rows)].astype(F32) + transit[k][s][(which, *kept_spot)].astype(F32)
                for spot, kept_spot in found
            ]
            for (spot, _), both in zip(found, sums):
                ys[(*spot, rows)] = both.astype(BF16)
            scatter_copy(k, s, q, 4 + which)

    def scatter_end(k, s, q):
        for which in range(2, 6):
            scatters[k, s, q, which].wait_recv()
        rows = pl.ds(*SCATTER_ROWS[k])
        found = each_block(k, s, q, 0)
        sums = [
            (
                ys[(*spot, rows)].astype(F32)
                + landing[k][s][(0, *kept_spot)].astype(F32)
                + landing[k][s][(1, *kept_spot)].astype(F32)
            ).astype(BF16)
            for spot, kept_spot in found
        ]
        for (spot, _), both in zip(found, sums):
            ys[(*spot, rows)] = both

    def near(q):
        for which in (2, 3):
            scatter_copy(0, 0, q, which)
            scatter_copy(1, 0, q, which)

    def last_copy(k, d):
        start, count = SCATTER_ROWS[k]
        axis = SCATTER_ORDER[k][2]
        copy = pltpu.make_async_remote_copy(
            src_ref=ys.at[(*block_index(on_axis(axis, d)), pl.ds(start, count))],
            dst_ref=landing[k][2].at[d - 1], send_sem=sc_s.at[k, 29 + d], recv_sem=sc_r.at[k, 29 + d],
            device_id=at(on_axis(axis, d), c), device_id_type=MESH,
        )
        copy.start()
        scatters[k, 2, 0, d] = copy

    for q in range(4):
        by = (y + GROUPS[q] + 4) % 4

        def project(bxh, _, by=by):
            col = pl.ds(pl.multiple_of((bxh * 4 + by) * 1024, 1024), 1024)
            wide = jnp.dot(hidden[...], down_all[:, col], preferred_element_type=F32)
            for pair in range(4):
                low = wide[:, pair * 128:(pair + 1) * 128]
                high = wide[:, 512 + pair * 128:512 + (pair + 1) * 128]
                first = jnp.where(lane_low, low, pltpu.roll(high, 64, 1)).astype(BF16)
                second = jnp.where(lane_low, pltpu.roll(low, 64, 1), high).astype(BF16)
                ys[pair // 2, (pair % 2) * 2, bxh, by] = first
                ys[pair // 2, (pair % 2) * 2 + 1, bxh, by] = second
            return 0

        lax.fori_loop(0, 2, project, 0)
        for which in range(2):
            scatter_copy(0, 0, q, which)
            scatter_copy(1, 0, q, which)
        for part in range(4):
            for which in ((0, 1), (3,), (2,), ())[q]:
                scatter_copy(2, 0, part, which)
    odd = h % 2
    tiles = []
    for core in range(2):
        window = pl.ds(pl.multiple_of(core * 512 + (h // 2) * 128, 128), 128)
        tiles.append(xs[:, :, xh, y, :, window].reshape(256, 128).astype(F32))
    even_pack = jnp.where(lane_low, tiles[0], pltpu.roll(tiles[1], 64, 1))
    odd_pack = jnp.where(lane_low, pltpu.roll(tiles[0], 64, 1), tiles[1])
    packed = jnp.where(odd == 0, even_pack, odd_pack)
    res_z[:, c] = packed.astype(BF16).reshape(8, 32, 128)
    res_copy = pltpu.make_async_remote_copy(
        src_ref=res_z.at[:, c], dst_ref=res_z.at[:, c], send_sem=fin_s.at[0], recv_sem=fin_r.at[0],
        device_id=sibling, device_id_type=MESH,
    )
    res_copy.start()

    near(0)
    for k in range(3):
        scatter_pass(k, 0, 0)
    near(1)
    for k in range(3):
        scatter_pass(k, 0, 1)
    near(2)
    for k in range(3):
        scatter_end(k, 0, 0)
        scatter_copy(k, 1, 0, 0)
        scatter_copy(k, 1, 0, 1)
    for k in range(3):
        scatter_pass(k, 0, 2)
    near(3)
    for k in range(3):
        scatter_end(k, 0, 1)
        scatter_copy(k, 1, 0, 3)
    for k in range(3):
        scatter_pass(k, 0, 3)
    for k in range(3):
        scatter_end(k, 0, 2)
        scatter_copy(k, 1, 0, 2)
    for k in range(3):
        scatter_pass(k, 1, 0)
    for k in range(3):
        scatter_end(k, 0, 3)
    for k in range(3):
        scatter_end(k, 1, 0)
        for d in (2, 1, 3):
            last_copy(k, d)
    for k in range(3):
        for i in range(1, 8):
            proj_copy(k, (h + i) % 8).wait_send()
    for copy in gathers.values():
        copy.wait_send()

    def give(i, copy, z_ref):
        copy.wait_send()
        copy.wait_recv()
        ordered = jnp.dot(perm[...], z_ref[...].reshape(512, 128), preferred_element_type=F32)
        ordered = jnp.where(c == 0, ordered, pltpu.roll(ordered, 64, 1))
        both_out[i] = ordered.T[0:64, :].astype(BF16)

    give(0, res_copy, res_z)
    for k in range(3):
        start, count = SCATTER_ROWS[k]
        sums = ys[(*block_index(me), pl.ds(start, count))].astype(F32)
        for d in range(1, 4):
            scatters[k, 2, 0, d].wait_recv()
            sums = sums + landing[k][2][d - 1].astype(F32)
        lay_z[start // 32:(start + count) // 32, c] = sums.astype(BF16).reshape(count // 32, 32, 128)
    lay_copy = pltpu.make_async_remote_copy(
        src_ref=lay_z.at[:, c], dst_ref=lay_z.at[:, c], send_sem=fin_s.at[1], recv_sem=fin_r.at[1],
        device_id=sibling, device_id_type=MESH,
    )
    lay_copy.start()
    for copy in scatters.values():
        copy.wait_send()
    give(1, lay_copy, lay_z)


def layer(query, new_key, new_value, lengths, gain, slots, *hbm_args):
    vmem = pl.BlockSpec(memory_space=pltpu.VMEM)
    smem = pl.BlockSpec(memory_space=pltpu.SMEM)
    hbm = pl.BlockSpec(memory_space=pl.ANY)
    dma = pltpu.SemaphoreType.DMA
    landing, transit = [], []
    for k in range(3):
        for s in range(3):
            kept, count = kept_shape(SCATTER_ORDER[k][s + 1:]), SCATTER_ROWS[k][1]
            landing.append(pltpu.VMEM((3 if s == 2 else 2, *kept, count, 128), BF16))
            if s < 2:
                transit.append(pltpu.VMEM((2, *kept, count // 2, 128), BF16))
    return pl.pallas_call(
        layer_kernel,
        out_shape=jax.ShapeDtypeStruct((2, 64, 512), BF16),
        in_specs=[vmem, vmem, vmem, smem, vmem, vmem] + [hbm] * len(hbm_args),
        out_specs=vmem,
        scratch_shapes=[
            pltpu.VMEM((RING, CTX, HD), BF16),
            pltpu.VMEM((RING, CTX, HD), BF16),
            pltpu.VMEM((2, UNROLL, PER_KV, CTX), F32),
            pltpu.VMEM((SLOTS, PER_KV, HD), F32),
            pltpu.VMEM((SLOTS, PER_KV, HD), F32),
            pltpu.VMEM((SLOTS, HD), F32),
            pltpu.VMEM((SLOTS, HD), F32),
            pltpu.VMEM((8, 128), F32),
            pltpu.VMEM((16, 8, 128), F32),
            pltpu.VMEM((8, 32, 1024), BF16),
            pltpu.VMEM((512, 512), BF16),
            pltpu.VMEM((512, 512), BF16),
            pltpu.VMEM((1024, 512), BF16),
            pltpu.VMEM((1024, 512), BF16),
            pltpu.VMEM((4 * HID, D), BF16),
            pltpu.VMEM((2 * HID, D), BF16),
            pltpu.VMEM((8, 32, 1024), BF16),
            pltpu.VMEM((8, 32, 1024), BF16),
            pltpu.VMEM((2, 4, 2, 4, 32, 1024), BF16),
            pltpu.VMEM((2, 4, 2, 4, 256, 128), BF16),
            pltpu.VMEM((4 * HID, 256), F32),
            pltpu.VMEM((256, 128), F32),
            pltpu.VMEM((512, 512), BF16),
            pltpu.VMEM((512, 128), F32),
            pltpu.VMEM((256, 2 * HID), BF16),
            pltpu.VMEM((8, 2, 32, 128), BF16),
            pltpu.VMEM((8, 2, 32, 128), BF16),
            pltpu.VMEM((32, 1024), F32),
            *landing,
            *transit,
            dma((2, RING)),
            dma((5,)),
            dma((5,)), dma((5,)),
            dma((2, 7)), dma((2, 7)),
            dma((15,)), dma((15,)),
            dma((3, 8)), dma((3, 8)),
            dma((3, 24)), dma((3, 24)),
            dma((3, 33)), dma((3, 33)),
            dma((2,)), dma((2,)),
        ],
        compiler_params=pltpu.CompilerParams(
            collective_id=0, has_side_effects=True, vmem_limit_bytes=58 * 2**20
        ),
        cost_estimate=pl.CostEstimate(flops=6 * 10**9, bytes_accessed=42 * 10**6, transcendentals=0),
        name="layer",
    )(query, new_key, new_value, lengths, gain, slots, *hbm_args)


def per_device(
    query,
    new_key,
    new_value,
    key_cache,
    value_cache,
    lengths,
    slot_row,
    resid,
    out_weight,
    norm_gain,
    gate_weight,
    up_weight,
    down_weight,
):
    both = layer(
        query, new_key, new_value, lengths, norm_gain.reshape(4, 128), slot_row[None, :],
        key_cache, value_cache, resid, out_weight, gate_weight.T, up_weight.T, down_weight,
    )
    return (both[0].T, both[1].T)


def solution(mesh):
    placed = (
        P("grp", "head"),
        P("grp", "head"),
        P("grp", "head"),
        P("grp", "head", None, None),
        P("grp", "head", None, None),
        P("grp"),
        P(),
        P(None, "grp"),
        P("head", "grp"),
        P("grp"),
        P(None, ("grp", "head")),
        P(None, ("grp", "head")),
        P(("grp", "head"), None),
    )
    return jax.shard_map(
        per_device,
        mesh=mesh,
        in_specs=placed,
        out_specs=(P(None, ("grp", "head")), P(None, ("grp", "head"))),
        check_vma=False,
    )
```
